256 devices in a mesh: expert: 32 (over x, z_lo, y), tensor: 8 (over z_hi, core).
Axes of the slice: x: 4, y: 4, z: 8 (z_hi: 4, z_lo: 2; z = z_hi * 2 + z_lo), core: 2. Of those that a mesh axis runs over, the one named last changes fastest.
Arguments:
- context: bfloat16 [8192, 4096], P('expert', 'tensor'), may hold values from -6 to 6
- output_weight: bfloat16 [4096, 2048], P('tensor'), may hold values from -0.09375 to 0.09375
- residual: bfloat16 [8192, 2048], P('expert'), may hold values from -6 to 6
- norm_gain: float32 [2048], replicated, may hold values from 0.5 to 1.5
- routes: int32 [8192, 8], P('expert'), may hold values from 0 to 127, all different within a row; in each aligned block of 256 rows (0 to 255, 256 to 511, ...) at most 20 rows name the same one
- gate_values: float32 [8192, 8], P('expert'), may hold values from 0.05 to 0.25
- gate_weight: bfloat16 [2048, 98304], P(None, ('expert', 'tensor')), may hold values from -0.125 to 0.125
- up_weight: bfloat16 [2048, 98304], P(None, ('expert', 'tensor')), may hold values from -0.125 to 0.125
- down_weight: bfloat16 [98304, 2048], P(('expert', 'tensor')), may hold values from -0.21875 to 0.21875
Outputs:
- layer_out: bfloat16 [8192, 2048], P(('expert', 'tensor'))
The draws below stay inside these ranges and needn't reach their ends.
Inputs may be any that keep to these rules, and one draw needn't show every extreme that they name: `routes`: in each aligned block of 256 rows (the tokens of one index of expert), no expert is named by more than 20 rows, a bound that some block reaches.
All inputs are finite; a program needn't handle non-finite values.
Results may differ from the reference program's by a relative error of at most 0.014.
Values may be sent and summed in bfloat16 or wider, within the bound.
A program may use at most 64 MiB of HBM per device.

```python
import math
import jax
import jax.numpy as jnp
import numpy as np
from jax import lax

D = 2048
HQ = 32
HD = 128
FFE = 768
TOPK = 8
HALVES = 2
TOK_GRP = 256
TOKENS = 8192
EXP_IDX = 4
EXPERTS = 128
CAP = 20
N_EXPERT = 32
N_TENSOR = 8


def block_levels(own_key, shape, pieces, low, high):
    level = 1.0
    for dim, parts in pieces:
        steps = jax.random.uniform(jax.random.fold_in(jax.random.fold_in(own_key, 6), dim), (parts,), jnp.float32, low / len(pieces), high / len(pieces))
        level = level * jnp.repeat(jnp.exp(steps), shape[dim] // parts).reshape((-1,) + (1,) * (len(shape) - 1 - dim))
    return level


def shared_out(key, own, number, rows, amount, top, bound, skew):
    order = jax.random.permutation(key, amount)
    heavy_load, usual = shares(amount, rows * top, bound, skew, True), shares(amount, rows * top, bound, skew, False)
    places = jnp.arange(amount)

    def named(sizes, turn):
        used = int((sizes > 0).sum())
        fixed = max(1, used // 4)
        passed = fixed + (places - fixed + turn * (used - fixed)) % max(1, amount - fixed)
        return jnp.zeros((amount,), jnp.int32).at[order[jnp.where(places < fixed, places, passed)]].set(jnp.asarray(sizes, jnp.int32))

    sizes = jnp.where(number % 4 == 0, named(heavy_load, number // 4), named(usual, number - number // 4 - 1))
    mixed = jax.random.permutation(jax.random.fold_in(own, 3), amount)
    giver, receiver = mixed[0:amount // 2 * 2:2], mixed[1:amount // 2 * 2:2]
    slack = jnp.minimum(sizes[giver] - 1, bound - sizes[receiver]) // 2
    slack = jnp.where((giver == order[0]) | (receiver == order[0]) | (sizes[receiver] == 0), 0, jnp.maximum(slack, 0))
    passed = jax.random.randint(jax.random.fold_in(own, 4), (amount // 2,), 0, 1 << 20) % (slack + 1)
    sizes = sizes.at[giver].add(-passed).at[receiver].add(passed)
    items = jnp.searchsorted(jnp.cumsum(sizes), jnp.arange(rows * top), side="right").astype(jnp.int32)
    listing = items.reshape(top, rows).T
    listing = listing[jax.random.permutation(jax.random.fold_in(own, 1), rows)]
    turn = jax.random.randint(jax.random.fold_in(own, 2), (rows, 1), 0, top)
    return jnp.take_along_axis(listing, (jnp.arange(top)[None, :] + turn) % top, axis=1)


def shares(count, total, most, lean, full):
    weights = [(1 << 20) // math.isqrt(rank ** lean) + 1 for rank in range(1, count + 1)]
    largest = most if full else min(most, max(-(-total // count), total * weights[0] // sum(weights)))
    least = 1 if total - largest >= count - 1 else 0
    holding, spare = [largest] + [least] * (count - 1), total - largest - least * (count - 1)
    while spare > 0:
        movable = [i for i in range(1, count) if holding[i] < largest] or [i for i in range(1, count) if holding[i] < most]
        pool, left = sum([weights[i] for i in movable]), spare
        for i in movable:
            addition = min(most - holding[i], max(1, left * weights[i] // pool), spare)
            holding[i] = holding[i] + addition
            spare = spare - addition
    return np.array(holding)


def centred(stream_key, extent, width, limit, shards=(), held_as=jnp.bfloat16):
    level = block_levels(stream_key, extent, shards, -0.22, 0.18) if shards else 1.0
    drawn = jax.random.normal(stream_key, extent, jnp.float32) * width * level
    return jnp.minimum(jnp.maximum(drawn, -limit), limit).astype(held_as)


def setup_inputs(seed: int = 0) -> dict:
    splits = jax.random.split(jax.random.key(seed), 10)
    context = centred(splits[0], (TOKENS, HQ * HD), 1.0, 6.0, ((0, 32), (1, 8)))
    output_weight = centred(splits[1], (HQ * HD, D), (HQ * HD) ** -0.5, 0.09375, ((0, 8),))
    residual = centred(splits[2], (TOKENS, D), 1.0, 6.0, ((0, 32),))
    norm_gain = jnp.clip(1.0 + 0.1 * jax.random.normal(splits[3], (D,), jnp.float32), 0.5, 1.5)
    routes_keys = jax.random.split(jax.random.fold_in(splits[4], 1), TOKENS // TOK_GRP)
    routes_turns = jax.random.permutation(jax.random.fold_in(splits[4], 3), TOKENS // TOK_GRP)
    routes = jax.vmap(lambda own, number: shared_out(jax.random.fold_in(splits[4], 2), own, number, TOK_GRP, EXPERTS, TOPK, CAP, 2))(routes_keys, routes_turns).reshape((TOKENS, TOPK))
    gate_values = jnp.clip(0.05 + 0.2 * jax.random.uniform(splits[5], (TOKENS, TOPK), jnp.float32) ** block_levels(splits[5], (TOKENS, TOPK), ((0, 32),), -0.2, 0.2), 0.05, 0.25)
    gate_weight = centred(splits[6], (D, EXPERTS * FFE), D ** -0.5, 0.125, ((1, 256),))
    up_weight = centred(splits[7], (D, EXPERTS * FFE), D ** -0.5, 0.125, ((1, 256),))
    down_weight = centred(splits[8], (EXPERTS * FFE, D), FFE ** -0.5, 0.21875, ((0, 256),))
    return dict(context=context, output_weight=output_weight, residual=residual, norm_gain=norm_gain, routes=routes, gate_values=gate_values, gate_weight=gate_weight, up_weight=up_weight, down_weight=down_weight)


def root_norm(values, norm_gain):
    squares = values * values
    inverse = lax.rsqrt(lax.optimization_barrier(jnp.mean(squares, axis=-1, keepdims=True)) + 1e-06)
    return (values * inverse * norm_gain).astype(jnp.bfloat16)

def reference(context, output_weight, residual, norm_gain, routes, gate_values, gate_weight, up_weight, down_weight):
    head_part = HQ * HD // N_TENSOR
    half_width = FFE // HALVES
    gate_experts = gate_weight.reshape(D, EXPERTS, FFE).transpose(1, 0, 2)
    up_experts = up_weight.reshape(D, EXPERTS, FFE).transpose(1, 0, 2)
    down_experts = down_weight.reshape(EXPERTS, FFE, D)
    parts_weight = output_weight.reshape(N_TENSOR, head_part, D)

    def one_group(inputs):
        group_context, group_residual, group_routes, group_gates = inputs
        head_total = jnp.zeros((TOK_GRP, D), jnp.float32)
        for part_index in range(N_TENSOR):
            head_piece = group_context[:, part_index * head_part:(part_index + 1) * head_part]
            rounded = jnp.dot(head_piece, parts_weight[part_index], preferred_element_type=jnp.float32).astype(jnp.bfloat16)
            rounded = lax.optimization_barrier(rounded)
            head_total = head_total + rounded.astype(jnp.float32)
        attention = (group_residual.astype(jnp.float32) + head_total).astype(jnp.bfloat16)
        normed = root_norm(attention.astype(jnp.float32), norm_gain)
        expert_ids = jnp.arange(EXPERTS, dtype=jnp.int32)
        expert_hits = lax.optimization_barrier(jnp.sum((group_routes[:, :, None] == expert_ids[None, None, :]).astype(jnp.int32), axis=1))
        rank_table = jnp.cumsum(expert_hits, axis=0) - expert_hits
        slot_index = jnp.take_along_axis(rank_table, group_routes, axis=1).astype(jnp.int32)
        token_ids = jnp.broadcast_to(jnp.arange(TOK_GRP, dtype=jnp.int32)[:, None], group_routes.shape)
        token_table = jnp.full((EXPERTS, CAP), TOK_GRP, jnp.int32).at[group_routes, slot_index].set(token_ids)
        padded = jnp.concatenate([normed, jnp.zeros((1, D), jnp.bfloat16)], axis=0)

        def one_expert(expert_inputs):
            rows_index, gate_block, up_block, down_block = expert_inputs
            slot_rows = jnp.take(padded, rows_index, axis=0)
            halves = []
            for half_index in range(HALVES):
                column_start = half_index * half_width
                gate_out = jnp.dot(slot_rows, gate_block[:, column_start:column_start + half_width], preferred_element_type=jnp.float32)
                up_out = jnp.dot(slot_rows, up_block[:, column_start:column_start + half_width], preferred_element_type=jnp.float32)
                activated = (jax.nn.silu(gate_out) * up_out).astype(jnp.bfloat16)
                halves.append(jnp.dot(activated, down_block[column_start:column_start + half_width], preferred_element_type=jnp.float32).astype(jnp.bfloat16))
            return jnp.stack(halves, axis=1)
        expert_out = lax.map(one_expert, (token_table, gate_experts, up_experts, down_experts))
        flat_out = expert_out.reshape(EXPERTS * CAP, HALVES, D)
        picked = jnp.take(flat_out, group_routes * CAP + slot_index, axis=0).astype(jnp.float32)
        class_base = group_routes % EXP_IDX * HALVES
        expert_sum = jnp.zeros((TOK_GRP, D), jnp.float32)
        for class_index in range(N_TENSOR):
            weights = jnp.stack([jnp.where(class_base + half_index == class_index, group_gates, jnp.zeros_like(group_gates)) for half_index in range(HALVES)], axis=2)
            class_term = jnp.einsum('gkh,gkhd->gd', weights, picked, precision=lax.Precision.HIGHEST).astype(jnp.bfloat16)
            class_term = lax.optimization_barrier(class_term)
            expert_sum = expert_sum + class_term.astype(jnp.float32)
        return (attention.astype(jnp.float32) + expert_sum).astype(jnp.bfloat16)
    layer_rows = lax.map(one_group, (context.reshape(N_EXPERT, TOK_GRP, HQ * HD), residual.reshape(N_EXPERT, TOK_GRP, D), routes.reshape(N_EXPERT, TOK_GRP, TOPK), gate_values.reshape(N_EXPERT, TOK_GRP, TOPK)))
    return layer_rows.reshape(N_EXPERT * TOK_GRP, D)
```

```python
import functools

import jax
import jax.numpy as jnp
from jax import lax
from jax.experimental import pallas as pl
from jax.experimental.pallas import tpu as pltpu
from jax.sharding import PartitionSpec as P

MESH = pl.DeviceIdType.MESH
NX, NY, NZ, NHI = 4, 4, 8, 4
PEERS = NX * NY
SLABS = 5
SLOTS = SLABS * 8
ROWS = PEERS * SLOTS
CHUNKS = 4
BF, F32 = jnp.bfloat16, jnp.float32


def dot(a, b):
    return jnp.dot(a, b, preferred_element_type=F32)


def kernel(
    ctx_h, ow_h, res_h, gain_h, routes_h, gates_h, gw_h, uw_h, dw_h, out_ref,
    ctx, ow, res, gain, routes, gates, wgu, wd, load_sem,
    hp_send, hp_recv, hp_ss, hp_rs, total,
    rs_send, rs_relay, rs_last, rs_ss, relay_rs, last_rs,
    table, table_ss, table_rs, pick, spread,
    att, sq_send, sq_recv, sq_ss, sq_rs,
    toks, ag_ss, ag_rs,
    pack, rows_own, rows_other, pack_ss, pack_rs, swap_ss, swap_rs,
    acc, act, y_send, y_recv, y_ss, y_rs,
    back, ret, back_ss, back_rs,
    part, sum_send, sum_recv, sum_ss, sum_rs,
    fin, fin_send, fin_recv, fin_ss, fin_rs,
):
    e, t = lax.axis_index("expert"), lax.axis_index("tensor")
    x, zl, y = e // (2 * NY), (e // NY) % 2, e % NY
    zh, c = t // 2, t % 2
    z = zh * 2 + zl
    group = ctx.shape[0]
    half = res.shape[1]
    cw = half // CHUNKS
    blk = group // NHI
    other = 1 - c

    def at_z(k):
        to = (z + k + NZ) % NZ
        return {"expert": (x * 2 + to % 2) * NY + y, "tensor": (to // 2) * 2 + c}

    def at_xy(i, sign):
        px = (x + sign * (i // NY) + NX) % NX
        py = (y + sign * (i % NY) + NY) % NY
        return {"expert": (px * 2 + zl) * NY + py, "tensor": t}

    core = {"expert": e, "tensor": zh * 2 + other}
    mate = {"expert": (x * 2 + (1 - zl)) * NY + y, "tensor": t}

    def place(k):
        to = (z + k + NZ) % NZ
        return (to % 2) * NHI + to // 2

    def send(src, dst, ss, rs, to):
        copy = pltpu.make_async_remote_copy(
            src_ref=src, dst_ref=dst, send_sem=ss, recv_sem=rs, device_id=to, device_id_type=MESH
        )
        copy.start()
        sent.append(copy)
        return copy

    sent = []

    loads = []

    def load(src, dst):
        copy = pltpu.make_async_copy(src, dst, load_sem.at[len(loads)])
        copy.start()
        loads.append(copy)
        return copy

    own_cols = pl.ds(pl.multiple_of(c * half, half), half)
    other_cols = pl.ds(pl.multiple_of(other * half, half), half)
    l_ctx = load(ctx_h, ctx)
    l_ow1 = load(ow_h.at[:, other_cols], ow.at[0])
    l_ow0 = load(ow_h.at[:, own_cols], ow.at[1])
    l_routes = load(routes_h, routes)
    l_gates = load(gates_h, gates)
    l_res = load(res_h.at[pl.ds(pl.multiple_of(zh * blk, blk), blk), own_cols], res)
    l_gain = load(gain_h.at[:, own_cols], gain)
    ffn = gw_h.shape[1]
    l_gw = load(gw_h, wgu.at[:, pl.ds(0, ffn)])
    l_uw = load(uw_h, wgu.at[:, pl.ds(ffn, ffn)])
    l_dw = load(dw_h, wd)

    barrier = pltpu.get_barrier_semaphore()

    def hello(i, carry):
        pl.semaphore_signal(barrier, inc=1, device_id=at_xy(i, 1), device_id_type=MESH)
        return carry

    lax.fori_loop(1, PEERS, hello, 0)
    for to in (at_z(1), at_z(-1), at_z(2), at_z(-2), core):
        pl.semaphore_signal(barrier, inc=1, device_id=to, device_id_type=MESH)

    l_routes.wait()
    l_gates.wait()
    eye = (
        lax.broadcasted_iota(jnp.int32, (8, 8), 0) == lax.broadcasted_iota(jnp.int32, (8, 8), 1)
    ).astype(F32).astype(BF)
    turn = (((1,), (1,)), ((), ()))
    table[zl, 0:8, :] = lax.dot_general(
        eye, routes[...].astype(F32).astype(BF), turn, preferred_element_type=F32
    )
    table[zl, 8:16, :] = lax.dot_general(
        eye, gates[...].astype(BF), turn, preferred_element_type=F32
    )

    l_ctx.wait()
    l_ow1.wait()
    for q in range(CHUNKS):
        hp_send[q] = dot(ctx[...], ow[0, :, q * cw : (q + 1) * cw]).astype(BF)
        if q == 0:
            pl.semaphore_wait(barrier, PEERS + 4)
        send(hp_send.at[q], hp_recv.at[q], hp_ss.at[q], hp_rs.at[q], core)
    mine = send(table.at[zl], table.at[zl], table_ss, table_rs, mate)
    l_ow0.wait()
    for q in range(CHUNKS):
        total[q] = dot(ctx[...], ow[1, :, q * cw : (q + 1) * cw])

    def rows_of(k):
        return pl.ds(pl.multiple_of(((zh + k + NHI) % NHI) * blk, blk), blk)

    left_first = CHUNKS // 2
    order = [q for pair in zip(range(left_first), range(left_first, CHUNKS)) for q in pair]
    hp_copies = list(sent[:CHUNKS])
    relays, lasts = {}, {}
    for q in order:
        way = 1 if q < left_first else -1
        hp_copies[q].wait_recv()
        total[q] = total[q] + hp_recv[q].astype(F32)
        rs_send[q, 0] = total[q, rows_of(2), :].astype(BF)
        relays[q] = send(rs_send.at[q, 0], rs_relay.at[q], rs_ss.at[q, 0], relay_rs.at[q], at_z(2 * way))
        rs_send[q, 1] = total[q, rows_of(-way), :].astype(BF)
        lasts[q, 1] = send(rs_send.at[q, 1], rs_last.at[q, 1], rs_ss.at[q, 1], last_rs.at[q, 1], at_z(-2 * way))

    mine.wait_recv()
    peer = lax.broadcasted_iota(jnp.int32, (PEERS, group), 0)
    px, py = (x + (peer >> 2)) & (NX - 1), (y + (peer & (NY - 1))) & (NY - 1)
    named = (((px * 2 + zl) * NY + py) * NHI + zh).astype(F32)
    earlier = (
        lax.broadcasted_iota(jnp.int32, (group, group), 0)
        < lax.broadcasted_iota(jnp.int32, (group, group), 1)
    ).astype(F32).astype(BF)
    slot = lax.broadcasted_iota(jnp.int32, (PEERS, SLOTS, group), 1).astype(F32)
    before = jnp.zeros((PEERS, 1), F32)
    for g in range(2):
        hit = jnp.zeros((PEERS, group), F32)
        weight = jnp.zeros((PEERS, group), F32)
        for k in range(8):
            same = table[g, k : k + 1, :] == named
            hit = hit + jnp.where(same, 1.0, 0.0)
            weight = weight + jnp.where(same, table[g, 8 + k : 9 + k, :], 0.0)
        rank = dot(hit.astype(BF), earlier) + before
        before = before + jnp.sum(hit, axis=1, keepdims=True)
        rank = jnp.where(hit > 0.0, rank, -1.0)
        chosen = slot == rank[:, None, :]
        pick[:, g * group : (g + 1) * group] = (
            jnp.where(chosen, 1.0, 0.0).reshape(ROWS, group).astype(BF)
        )
        gated = jnp.where(chosen, jnp.broadcast_to(weight[:, None, :], chosen.shape), 0.0)
        spread[g * group : (g + 1) * group, :] = gated.reshape(ROWS, group).T.astype(BF)

    for q in order:
        way = 1 if q < left_first else -1
        relays[q].wait_recv()
        rs_send[q, 2] = (total[q, rows_of(way), :] + rs_relay[q].astype(F32)).astype(BF)
        lasts[q, 0] = send(rs_send.at[q, 2], rs_last.at[q, 0], rs_ss.at[q, 2], last_rs.at[q, 0], at_z(2 * way))

    l_res.wait()
    l_gain.wait()
    squares = jnp.zeros((blk, 1), F32)
    for q in order:
        lasts[q, 1].wait_recv()
        lasts[q, 0].wait_recv()
        summed = total[q, rows_of(0), :] + rs_last[q, 0].astype(F32) + rs_last[q, 1].astype(F32)
        attention = (res[:, q * cw : (q + 1) * cw].astype(F32) + summed).astype(BF)
        att[q] = attention
        wide = attention.astype(F32)
        squares = squares + jnp.sum(wide * wide, axis=1, keepdims=True)
    sq_send[...] = jnp.broadcast_to(squares, sq_send.shape)
    send(sq_send, sq_recv, sq_ss, sq_rs, core).wait_recv()
    mean = (squares + sq_recv[:, 0:1]) / (2 * half)
    inverse = lax.rsqrt(mean + 1e-06)

    def steps(q):
        return (4, 3) if q < left_first else (3, 4)

    ways = (1, -1)
    for q in range(CHUNKS):
        toks[q, place(0)] = (
            att[q].astype(F32) * inverse * gain[:, q * cw : (q + 1) * cw]
        ).astype(BF)
    gathers = {}
    packs = {}

    def to_peers(src, dst, ss, rs, q, sign):
        def one(i, carry):
            pltpu.make_async_remote_copy(
                src_ref=src.at[q, pl.ds(i * SLABS, SLABS)],
                dst_ref=dst.at[q, pl.ds(i * SLABS, SLABS)],
                send_sem=ss.at[q], recv_sem=rs.at[q],
                device_id=at_xy(i, sign), device_id_type=MESH,
            ).start()
            return carry

        lax.fori_loop(1, PEERS, one, 0)
        rest = pl.ds(SLABS, (PEERS - 1) * SLABS)
        copy = pltpu.make_async_remote_copy(
            src_ref=src.at[q, rest], dst_ref=dst.at[q, rest],
            send_sem=ss.at[q], recv_sem=rs.at[q],
            device_id=at_xy(1, sign), device_id_type=MESH,
        )
        sent.append(copy)
        return copy

    for tick in range(CHUNKS + NZ // 2):
        for q in range(CHUNKS):
            s = tick - q
            if s < 0 or s > NZ // 2:
                continue
            for d, way in enumerate(ways):
                if s >= 1 and s - 1 < steps(q)[d]:
                    gathers[q, d, s - 1].wait_recv()
                if s < steps(q)[d]:
                    there = toks.at[q, place(-way * s)]
                    gathers[q, d, s] = send(there, there, ag_ss.at[q, d, s], ag_rs.at[q, d, s], at_z(way))
            if s == NZ // 2:
                picked = dot(pick[...], toks[q].reshape(2 * group, cw)).astype(BF)
                picked = picked.reshape(PEERS * SLABS, 8, cw)
                rows_own[q, 0:SLABS] = picked[0:SLABS]
                pack[q, SLABS:] = picked[SLABS:]
                packs[q] = to_peers(pack, rows_own, pack_ss, pack_rs, q, 1)

    l_gw.wait()
    l_uw.wait()
    l_dw.wait()

    def into(rows, q, side):
        k0 = pl.multiple_of(side * half + q * cw, cw)
        return dot(rows[q].reshape(ROWS, cw), wgu[pl.ds(k0, cw), :])

    swaps = {}
    for q in range(CHUNKS):
        packs[q].wait_recv()
        swaps[q] = send(rows_own.at[q], rows_other.at[q], swap_ss.at[q], swap_rs.at[q], core)
        if q == 0:
            acc[...] = into(rows_own, q, c)
        else:
            acc[...] = acc[...] + into(rows_own, q, c)
            swaps[q - 1].wait_recv()
            acc[...] = acc[...] + into(rows_other, q - 1, other)
    swaps[CHUNKS - 1].wait_recv()
    acc[...] = acc[...] + into(rows_other, CHUNKS - 1, other)

    gate = acc[:, 0:ffn]
    act[...] = (gate / (1.0 + jnp.exp(-gate)) * acc[:, ffn : 2 * ffn]).astype(BF)

    crossing, backs = {}, {}

    def out_of(q, side):
        n0 = pl.multiple_of(side * half + q * cw, cw)
        return dot(act[...], wd[:, pl.ds(n0, cw)])

    def cross(q):
        y_send[q] = out_of(q, other).astype(BF)
        crossing[q] = send(y_send.at[q], y_recv.at[q], y_ss.at[q], y_rs.at[q], core)

    cross(0)
    for q in range(CHUNKS):
        if q + 1 < CHUNKS:
            cross(q + 1)
        own = out_of(q, c)
        crossing[q].wait_recv()
        both = (own + y_recv[q].astype(F32)).astype(BF).reshape(PEERS * SLABS, 8, cw)
        ret[q, 0:SLABS] = both[0:SLABS]
        back[q, SLABS:] = both[SLABS:]
        backs[q] = to_peers(back, ret, back_ss, back_rs, q, -1)

    sums = {}
    for tick in range(CHUNKS + NZ // 2):
        for q in range(CHUNKS):
            s = tick - q
            if s < 0 or s > NZ // 2:
                continue
            if s == 0:
                backs[q].wait_recv()
                part[q] = dot(spread[...], ret[q].reshape(ROWS, cw)).reshape(NZ, blk, cw)
            for d, way in enumerate(ways):
                n = steps(q)[d]
                if s >= 1 and s - 1 < n:
                    sums[q, d, s - 1].wait_recv()
                if s < n:
                    value = part[q, place(way * (n - s))]
                    if s >= 1:
                        value = value + sum_recv[q, d, s - 1].astype(F32)
                    sum_send[q, d, s] = value.astype(BF)
                    sums[q, d, s] = send(
                        sum_send.at[q, d, s], sum_recv.at[q, d, s], sum_ss.at[q, d, s], sum_rs.at[q, d, s], at_z(way)
                    )
            if s == NZ // 2:
                value = part[q, place(0)]
                for d in range(2):
                    value = value + sum_recv[q, d, steps(q)[d] - 1].astype(F32)
                fin[:, q * cw : (q + 1) * cw] = (att[q].astype(F32) + value).astype(BF)

    few = blk // 2
    keep = pl.ds(pl.multiple_of(c * few, few), few)
    give = pl.ds(pl.multiple_of(other * few, few), few)
    fin_send[...] = fin[give, :]
    last = send(fin_send, fin_recv, fin_ss, fin_rs, core)
    out_ref[:, own_cols] = fin[keep, :]
    last.wait_recv()
    out_ref[:, other_cols] = fin_recv[...]
    for copy in sent:
        copy.wait_send()


def local(context, output_weight, residual, norm_gain, routes, gate_values, gate_weight, up_weight, down_weight):
    group, heads = context.shape
    width = residual.shape[1]
    half = width // 2
    cw = half // CHUNKS
    blk = group // NHI
    ffn = gate_weight.shape[1]
    dma = pltpu.SemaphoreType.DMA
    vm = pltpu.VMEM
    q = CHUNKS
    steps = NZ // 2
    scratch = [
        vm((group, heads), BF), vm((2, heads, half), BF), vm((blk, half), BF), vm((1, half), F32),
        vm(routes.shape, jnp.int32), vm(gate_values.shape, F32), vm((width, 2 * ffn), BF), vm((ffn, width), BF), dma((10,)),
        vm((q, group, cw), BF), vm((q, group, cw), BF), dma((q,)), dma((q,)), vm((q, group, cw), F32),
        vm((q, 3, blk, cw), BF), vm((q, blk, cw), BF), vm((q, 2, blk, cw), BF), dma((q, 3)), dma((q,)), dma((q, 2)),
        vm((2, 16, group), F32), dma(()), dma(()), vm((ROWS, 2 * group), BF), vm((2 * group, ROWS), BF),
        vm((q, blk, cw), BF), vm((blk, 128), F32), vm((blk, 128), F32), dma(()), dma(()),
        vm((q, NZ, blk, cw), BF), dma((q, 2, steps)), dma((q, 2, steps)),
        vm((q, PEERS * SLABS, 8, cw), BF), vm((q, PEERS * SLABS, 8, cw), BF), vm((q, PEERS * SLABS, 8, cw), BF),
        dma((q,)), dma((q,)), dma((q,)), dma((q,)),
        vm((ROWS, 2 * ffn), F32), vm((ROWS, ffn), BF), vm((q, ROWS, cw), BF), vm((q, ROWS, cw), BF), dma((q,)), dma((q,)),
        vm((q, PEERS * SLABS, 8, cw), BF), vm((q, PEERS * SLABS, 8, cw), BF), dma((q,)), dma((q,)),
        vm((q, NZ, blk, cw), F32), vm((q, 2, steps, blk, cw), BF), vm((q, 2, steps, blk, cw), BF),
        dma((q, 2, steps)), dma((q, 2, steps)),
        vm((blk, half), BF), vm((blk // 2, half), BF), vm((blk // 2, half), BF), dma(()), dma(()),
    ]
    return pl.pallas_call(
        kernel,
        out_shape=jax.ShapeDtypeStruct((blk // 2, width), BF),
        in_specs=[pl.BlockSpec(memory_space=pl.ANY)] * 9,
        out_specs=pl.BlockSpec(memory_space=pltpu.VMEM),
        scratch_shapes=scratch,
        compiler_params=pltpu.CompilerParams(
            collective_id=0, has_side_effects=True, vmem_limit_bytes=56 * 2**20
        ),
        cost_estimate=pl.CostEstimate(flops=4 * 10**9, bytes_accessed=10**7, transcendentals=0),
    )(context, output_weight, residual, norm_gain.reshape(1, -1), routes, gate_values, gate_weight, up_weight, down_weight)


def solution(mesh):
    in_specs = (
        P("expert", "tensor"),
        P("tensor", None),
        P("expert", None),
        P(),
        P("expert", None),
        P("expert", None),
        P(None, ("expert", "tensor")),
        P(None, ("expert", "tensor")),
        P(("expert", "tensor"), None),
    )
    out_specs = P(("expert", "tensor"), None)
    return jax.shard_map(local, mesh=mesh, in_specs=in_specs, out_specs=out_specs, check_vma=False)
```

```python
import functools

import jax
import jax.numpy as jnp
from jax import lax
from jax.experimental import pallas as pl
from jax.experimental.pallas import tpu as pltpu
from jax.sharding import PartitionSpec as P

MESH = pl.DeviceIdType.MESH
NX, NY, NZ, NHI = 4, 4, 8, 4
PEERS = NX * NY
SLABS = 5
SLOTS = SLABS * 8
ROWS = PEERS * SLOTS
CHUNKS = 4
BF, F32 = jnp.bfloat16, jnp.float32


def dot(a, b):
    return jnp.dot(a, b, preferred_element_type=F32)


def kernel(
    ctx_h, ow_h, res_h, gain_h, routes_h, gates_h, gw_h, uw_h, dw_h, out_ref,
    ctx, ow, res, gain, wgu, wd, load_sem,
    hp_send, hp_recv, hp_ss, hp_rs, total,
    rs_send, rs_relay, rs_last, rs_ss, relay_rs, last_rs,
    names, gates, table_ss, table_rs, pick, spread,
    att, sq_send, sq_recv, sq_ss, sq_rs,
    toks, near_ss, near_rs, far_ss, far_rs,
    pack, rows_own, rows_other, pack_ss, pack_rs, swap_ss, swap_rs,
    acc, act, y_send, y_recv, y_ss, y_rs,
    back, ret, back_ss, back_rs,
    part, far_send, far_recv, farsum_ss, farsum_rs, near_send, near_recv, nearsum_ss, nearsum_rs,
    fin, fin_send, fin_recv, fin_ss, fin_rs,
):
    e, t = lax.axis_index("expert"), lax.axis_index("tensor")
    x, zl, y = e // (2 * NY), (e // NY) % 2, e % NY
    zh, c = t // 2, t % 2
    z = zh * 2 + zl
    group = ctx.shape[0]
    half = res.shape[1]
    cw = half // CHUNKS
    blk = group // NHI
    other = 1 - c

    def at_z(k):
        to = (z + k + NZ) % NZ
        return {"expert": (x * 2 + to % 2) * NY + y, "tensor": (to // 2) * 2 + c}

    def at_xy(i, sign):
        px = (x + sign * (i // NY) + NX) % NX
        py = (y + sign * (i % NY) + NY) % NY
        return {"expert": (px * 2 + zl) * NY + py, "tensor": t}

    core = {"expert": e, "tensor": zh * 2 + other}
    mate = {"expert": (x * 2 + (1 - zl)) * NY + y, "tensor": t}

    def place(k):
        to = (z + k + NZ) % NZ
        return (to % 2) * NHI + to // 2

    def send(src, dst, ss, rs, to):
        copy = pltpu.make_async_remote_copy(
            src_ref=src, dst_ref=dst, send_sem=ss, recv_sem=rs, device_id=to, device_id_type=MESH
        )
        copy.start()
        sent.append(copy)
        return copy

    sent = []

    loads = []

    def load(src, dst):
        copy = pltpu.make_async_copy(src, dst, load_sem.at[len(loads)])
        copy.start()
        loads.append(copy)
        return copy

    own_cols = pl.ds(pl.multiple_of(c * half, half), half)
    other_cols = pl.ds(pl.multiple_of(other * half, half), half)
    l_ctx = load(ctx_h, ctx)
    l_ow1 = load(ow_h.at[:, other_cols], ow.at[0])
    l_ow0 = load(ow_h.at[:, own_cols], ow.at[1])
    l_routes = load(routes_h, names.at[zl])
    l_gates = load(gates_h, gates.at[zl])
    l_res = load(res_h.at[pl.ds(pl.multiple_of(zh * blk, blk), blk), own_cols], res)
    l_gain = load(gain_h.at[:, own_cols], gain)
    ffn = gw_h.shape[1]
    l_gw = load(gw_h, wgu.at[:, pl.ds(0, ffn)])
    l_uw = load(uw_h, wgu.at[:, pl.ds(ffn, ffn)])
    l_dw = load(dw_h, wd)

    barrier = pltpu.get_barrier_semaphore()

    def hello(i, carry):
        pl.semaphore_signal(barrier, inc=1, device_id=at_xy(i, 1), device_id_type=MESH)
        return carry

    lax.fori_loop(1, PEERS, hello, 0)
    for to in (at_z(1), at_z(-1), at_z(2), at_z(-2), core):
        pl.semaphore_signal(barrier, inc=1, device_id=to, device_id_type=MESH)

    l_ctx.wait()
    l_ow1.wait()
    for q in range(CHUNKS):
        hp_send[q] = dot(ctx[...], ow[0, :, q * cw : (q + 1) * cw]).astype(BF)
        if q == 0:
            pl.semaphore_wait(barrier, PEERS + 4)
        send(hp_send.at[q], hp_recv.at[q], hp_ss.at[q], hp_rs.at[q], core)
    l_routes.wait()
    l_gates.wait()
    tables = [
        send(names.at[zl], names.at[zl], table_ss.at[0], table_rs.at[0], mate),
        send(gates.at[zl], gates.at[zl], table_ss.at[1], table_rs.at[1], mate),
    ]
    l_ow0.wait()

    def rows_of(k):
        return pl.ds(pl.multiple_of(((zh + k + NHI) % NHI) * blk, blk), blk)

    left_first = CHUNKS // 2
    order = [q for pair in zip(range(left_first), range(left_first, CHUNKS)) for q in pair]
    hp_copies = list(sent[:CHUNKS])
    relays, lasts = {}, {}
    for q in order:
        way = 1 if q < left_first else -1
        own = dot(ctx[...], ow[1, :, q * cw : (q + 1) * cw])
        hp_copies[q].wait_recv()
        total[q] = own + hp_recv[q].astype(F32)
        rs_send[q, 0] = total[q, rows_of(2), :].astype(BF)
        relays[q] = send(rs_send.at[q, 0], rs_relay.at[q], rs_ss.at[q, 0], relay_rs.at[q], at_z(2 * way))
        rs_send[q, 1] = total[q, rows_of(-way), :].astype(BF)
        lasts[q, 1] = send(rs_send.at[q, 1], rs_last.at[q, 1], rs_ss.at[q, 1], last_rs.at[q, 1], at_z(-2 * way))

    for copy in tables:
        copy.wait_recv()
    peer = lax.broadcasted_iota(jnp.int32, (PEERS, group), 0)
    px, py = (x + (peer >> 2)) & (NX - 1), (y + (peer & (NY - 1))) & (NY - 1)
    named = ((px * 2 + zl) * NY + py) * NHI + zh
    earlier = (
        lax.broadcasted_iota(jnp.int32, (group, group), 0)
        < lax.broadcasted_iota(jnp.int32, (group, group), 1)
    ).astype(F32).astype(BF)
    slot = lax.broadcasted_iota(jnp.int32, (PEERS, SLOTS, group), 1).astype(F32)
    before = jnp.zeros((PEERS, 1), F32)
    for g in range(2):
        hit = jnp.zeros((PEERS, group), F32)
        weight = jnp.zeros((PEERS, group), F32)
        for k in range(names.shape[1]):
            same = names[g, k : k + 1, :] == named
            hit = hit + jnp.where(same, 1.0, 0.0)
            weight = weight + jnp.where(same, gates[g, k : k + 1, :], 0.0)
        rank = dot(hit.astype(BF), earlier) + before
        before = before + jnp.sum(hit, axis=1, keepdims=True)
        rank = jnp.where(hit > 0.0, rank, -1.0)
        chosen = slot == rank[:, None, :]
        pick[:, g * group : (g + 1) * group] = (
            jnp.where(chosen, 1.0, 0.0).reshape(ROWS, group).astype(BF)
        )
        gated = jnp.where(chosen, jnp.broadcast_to(weight[:, None, :], chosen.shape), 0.0)
        spread[g * group : (g + 1) * group, :] = gated.reshape(ROWS, group).T.astype(BF)

    for q in order:
        way = 1 if q < left_first else -1
        relays[q].wait_recv()
        rs_send[q, 2] = (total[q, rows_of(way), :] + rs_relay[q].astype(F32)).astype(BF)
        lasts[q, 0] = send(rs_send.at[q, 2], rs_last.at[q, 0], rs_ss.at[q, 2], last_rs.at[q, 0], at_z(2 * way))

    l_res.wait()
    l_gain.wait()
    squares = jnp.zeros((blk, 1), F32)
    for q in order:
        lasts[q, 1].wait_recv()
        lasts[q, 0].wait_recv()
        summed = total[q, rows_of(0), :] + rs_last[q, 0].astype(F32) + rs_last[q, 1].astype(F32)
        attention = (res[:, q * cw : (q + 1) * cw].astype(F32) + summed).astype(BF)
        att[q] = attention
        wide = attention.astype(F32)
        squares = squares + jnp.sum(wide * wide, axis=1, keepdims=True)
    sq_send[...] = jnp.broadcast_to(squares, sq_send.shape)
    send(sq_send, sq_recv, sq_ss, sq_rs, core).wait_recv()
    mean = (squares + sq_recv[:, 0:1]) / (2 * half)
    inverse = lax.rsqrt(mean + 1e-06)

    def opposite(q, d):
        return (q < left_first) == (d == 0)

    ways = (1, -1)
    for q in range(CHUNKS):
        toks[q, place(0)] = (
            att[q].astype(F32) * inverse * gain[:, q * cw : (q + 1) * cw]
        ).astype(BF)
    gathers = {}
    packs = {}

    def to_peers(src, dst, ss, rs, q, sign):
        def one(i, carry):
            pltpu.make_async_remote_copy(
                src_ref=src.at[q, pl.ds(i * SLABS, SLABS)],
                dst_ref=dst.at[q, pl.ds(i * SLABS, SLABS)],
                send_sem=ss.at[q], recv_sem=rs.at[q],
                device_id=at_xy(i, sign), device_id_type=MESH,
            ).start()
            return carry

        lax.fori_loop(1, PEERS, one, 0)
        rest = pl.ds(SLABS, (PEERS - 1) * SLABS)
        copy = pltpu.make_async_remote_copy(
            src_ref=src.at[q, rest], dst_ref=dst.at[q, rest],
            send_sem=ss.at[q], recv_sem=rs.at[q],
            device_id=at_xy(1, sign), device_id_type=MESH,
        )
        sent.append(copy)
        return copy

    def spread_own(q):
        block = toks.at[q, place(0)]
        for n in (2, 1):
            for d, way in enumerate(ways):
                gathers[q, d, n] = send(
                    block, block, near_ss.at[q, d, n - 1], near_rs.at[q, d, n - 1], at_z(n * way)
                )

    def pass_on(q):
        for d, way in enumerate(ways):
            gathers[q, d, 2].wait_recv()
            block = toks.at[q, place(-2 * way)]
            for n in (2, 1) if opposite(q, d) else (1,):
                gathers[q, d, 2 + n] = send(
                    block, block, far_ss.at[q, d, n - 1], far_rs.at[q, d, n - 1], at_z(n * way)
                )

    def dispatch(q):
        for d in range(2):
            for n in (1, 3, 4) if opposite(q, d) else (1, 3):
                gathers[q, d, n].wait_recv()
        picked = dot(pick[...], toks[q].reshape(2 * group, cw)).astype(BF)
        picked = picked.reshape(PEERS * SLABS, 8, cw)
        rows_own[q, 0:SLABS] = picked[0:SLABS]
        pack[q, SLABS:] = picked[SLABS:]
        packs[q] = to_peers(pack, rows_own, pack_ss, pack_rs, q, 1)

    spread_own(0)
    spread_own(1)
    for q in range(CHUNKS):
        pass_on(q)
        if q + 2 < CHUNKS:
            spread_own(q + 2)
        if q:
            dispatch(q - 1)
    dispatch(CHUNKS - 1)

    l_gw.wait()
    l_uw.wait()
    l_dw.wait()

    def into(rows, q, side):
        k0 = pl.multiple_of(side * half + q * cw, cw)
        return dot(rows[q].reshape(ROWS, cw), wgu[pl.ds(k0, cw), :])

    swaps = {}
    for q in range(CHUNKS):
        packs[q].wait_recv()
        swaps[q] = send(rows_own.at[q], rows_other.at[q], swap_ss.at[q], swap_rs.at[q], core)
        if q == 0:
            acc[...] = into(rows_own, q, c)
        else:
            acc[...] = acc[...] + into(rows_own, q, c)
            swaps[q - 1].wait_recv()
            acc[...] = acc[...] + into(rows_other, q - 1, other)
    swaps[CHUNKS - 1].wait_recv()
    acc[...] = acc[...] + into(rows_other, CHUNKS - 1, other)

    gate = acc[:, 0:ffn]
    act[...] = (gate / (1.0 + jnp.exp(-gate)) * acc[:, ffn : 2 * ffn]).astype(BF)

    crossing, backs = {}, {}

    def out_of(q, side):
        n0 = pl.multiple_of(side * half + q * cw, cw)
        return dot(act[...], wd[:, pl.ds(n0, cw)])

    def cross(q):
        y_send[q] = out_of(q, other).astype(BF)
        crossing[q] = send(y_send.at[q], y_recv.at[q], y_ss.at[q], y_rs.at[q], core)

    cross(0)
    for q in range(CHUNKS):
        if q + 1 < CHUNKS:
            cross(q + 1)
        own = out_of(q, c)
        crossing[q].wait_recv()
        both = (own + y_recv[q].astype(F32)).astype(BF).reshape(PEERS * SLABS, 8, cw)
        ret[q, 0:SLABS] = both[0:SLABS]
        back[q, SLABS:] = both[SLABS:]
        backs[q] = to_peers(back, ret, back_ss, back_rs, q, -1)

    sums = {}

    def combine(q):
        backs[q].wait_recv()
        part[q] = dot(spread[...], ret[q].reshape(ROWS, cw)).reshape(NZ, blk, cw)
        for d, way in enumerate(ways):
            for n in (2, 1) if opposite(q, d) else (1,):
                far_send[q, d, n - 1] = part[q, place((2 + n) * way)].astype(BF)
                sums[q, d, 2 + n] = send(
                    far_send.at[q, d, n - 1], far_recv.at[q, d, n - 1],
                    farsum_ss.at[q, d, n - 1], farsum_rs.at[q, d, n - 1], at_z(n * way),
                )
            near_send[q, d, 0] = part[q, place(way)].astype(BF)
            sums[q, d, 1] = send(
                near_send.at[q, d, 0], near_recv.at[q, d, 0],
                nearsum_ss.at[q, d, 0], nearsum_rs.at[q, d, 0], at_z(way),
            )

    def add_on(q):
        for d, way in enumerate(ways):
            value = part[q, place(2 * way)]
            for n in (2, 1) if opposite(q, d) else (1,):
                sums[q, d, 2 + n].wait_recv()
                value = value + far_recv[q, d, n - 1].astype(F32)
            near_send[q, d, 1] = value.astype(BF)
            sums[q, d, 2] = send(
                near_send.at[q, d, 1], near_recv.at[q, d, 1],
                nearsum_ss.at[q, d, 1], nearsum_rs.at[q, d, 1], at_z(2 * way),
            )

    def finish(q):
        value = part[q, place(0)]
        for d in range(2):
            for n in (1, 2):
                sums[q, d, n].wait_recv()
                value = value + near_recv[q, d, n - 1].astype(F32)
        fin[:, q * cw : (q + 1) * cw] = (att[q].astype(F32) + value).astype(BF)

    for q in range(CHUNKS):
        combine(q)
        if q:
            add_on(q - 1)
    add_on(CHUNKS - 1)
    for q in range(CHUNKS):
        finish(q)

    few = blk // 2
    keep = pl.ds(pl.multiple_of(c * few, few), few)
    give = pl.ds(pl.multiple_of(other * few, few), few)
    fin_send[...] = fin[give, :]
    last = send(fin_send, fin_recv, fin_ss, fin_rs, core)
    out_ref[:, own_cols] = fin[keep, :]
    last.wait_recv()
    out_ref[:, other_cols] = fin_recv[...]
    for copy in sent:
        copy.wait_send()


def local(context, output_weight, residual, norm_gain, routes, gate_values, gate_weight, up_weight, down_weight):
    group, heads = context.shape
    width = residual.shape[1]
    half = width // 2
    cw = half // CHUNKS
    blk = group // NHI
    ffn = gate_weight.shape[1]
    topk = routes.shape[1]
    dma = pltpu.SemaphoreType.DMA
    vm = pltpu.VMEM
    q = CHUNKS
    scratch = [
        vm((group, heads), BF), vm((2, heads, half), BF), vm((blk, half), BF), vm((1, half), F32),
        vm((width, 2 * ffn), BF), vm((ffn, width), BF), dma((10,)),
        vm((q, group, cw), BF), vm((q, group, cw), BF), dma((q,)), dma((q,)), vm((q, group, cw), F32),
        vm((q, 3, blk, cw), BF), vm((q, blk, cw), BF), vm((q, 2, blk, cw), BF), dma((q, 3)), dma((q,)), dma((q, 2)),
        vm((2, topk, group), jnp.int32), vm((2, topk, group), F32), dma((2,)), dma((2,)), vm((ROWS, 2 * group), BF), vm((2 * group, ROWS), BF),
        vm((q, blk, cw), BF), vm((blk, 128), F32), vm((blk, 128), F32), dma(()), dma(()),
        vm((q, NZ, blk, cw), BF), dma((q, 2, 2)), dma((q, 2, 2)), dma((q, 2, 2)), dma((q, 2, 2)),
        vm((q, PEERS * SLABS, 8, cw), BF), vm((q, PEERS * SLABS, 8, cw), BF), vm((q, PEERS * SLABS, 8, cw), BF),
        dma((q,)), dma((q,)), dma((q,)), dma((q,)),
        vm((ROWS, 2 * ffn), F32), vm((ROWS, ffn), BF), vm((q, ROWS, cw), BF), vm((q, ROWS, cw), BF), dma((q,)), dma((q,)),
        vm((q, PEERS * SLABS, 8, cw), BF), vm((q, PEERS * SLABS, 8, cw), BF), dma((q,)), dma((q,)),
        vm((q, NZ, blk, cw), F32),
        vm((q, 2, 2, blk, cw), BF), vm((q, 2, 2, blk, cw), BF), dma((q, 2, 2)), dma((q, 2, 2)),
        vm((q, 2, 2, blk, cw), BF), vm((q, 2, 2, blk, cw), BF), dma((q, 2, 2)), dma((q, 2, 2)),
        vm((blk, half), BF), vm((blk // 2, half), BF), vm((blk // 2, half), BF), dma(()), dma(()),
    ]
    return pl.pallas_call(
        kernel,
        out_shape=jax.ShapeDtypeStruct((blk // 2, width), BF),
        in_specs=[pl.BlockSpec(memory_space=pl.ANY)] * 9,
        out_specs=pl.BlockSpec(memory_space=pltpu.VMEM),
        scratch_shapes=scratch,
        compiler_params=pltpu.CompilerParams(
            collective_id=0, has_side_effects=True, vmem_limit_bytes=56 * 2**20
        ),
        cost_estimate=pl.CostEstimate(flops=4 * 10**9, bytes_accessed=10**7, transcendentals=0),
    )(context, output_weight, residual, norm_gain.reshape(1, -1), routes.T, gate_values.T, gate_weight, up_weight, down_weight)


def solution(mesh):
    in_specs = (
        P("expert", "tensor"),
        P("tensor", None),
        P("expert", None),
        P(),
        P("expert", None),
        P("expert", None),
        P(None, ("expert", "tensor")),
        P(None, ("expert", "tensor")),
        P(("expert", "tensor"), None),
    )
    out_specs = P(("expert", "tensor"), None)
    return jax.shard_map(local, mesh=mesh, in_specs=in_specs, out_specs=out_specs, check_vma=False)
```

```python
import functools

import jax
import jax.numpy as jnp
from jax import lax
from jax.experimental import pallas as pl
from jax.experimental.pallas import tpu as pltpu
from jax.sharding import PartitionSpec as P

MESH = pl.DeviceIdType.MESH
NX, NY, NZ, NHI = 4, 4, 8, 4
PEERS = NX * NY
SLABS = 5
SLOTS = SLABS * 8
ROWS = PEERS * SLOTS
OUT = ((0, 128), (128, 256), (384, 256), (640, 256), (896, 128))
BACK = ((0, 256), (256, 256), (512, 256), (768, 128), (896, 128))
OUT_DIRECT = (0,)
BACK_DIRECT = (4,)
RING = (1, -1, 2, -2, 3, -3, 4)
BF, F32 = jnp.bfloat16, jnp.float32


def dot(a, b):
    return jnp.dot(a, b, preferred_element_type=F32)


def kernel(
    ctx_h, ow_h, res_h, gain_h, routes_h, gates_h, gw_h, uw_h, dw_h, out_ref,
    ctx, ow, res, gain, wgu, wd, load_sem,
    hp_send, hp_recv, hp_ss, hp_rs, total,
    rs_send, rs_relay, rs_last, rs_ss, relay_rs, last_rs,
    names, gates, table_ss, table_rs, pick, spread,
    toks, near_ss, near_rs, far_ss, far_rs, all_ss, all_rs,
    pack, rows_own, rows_other, pack_ss, pack_rs, swap_ss, swap_rs,
    acc, square, act, y_send, y_recv, y_ss, y_rs,
    back, ret, back_ss, back_rs,
    part, far_send, far_recv, farsum_ss, farsum_rs, near_send, near_recv, nearsum_ss, nearsum_rs,
    all_send, all_recv, allsum_ss, allsum_rs,
    fin, fin_send, fin_recv, fin_ss, fin_rs,
):
    e, t = lax.axis_index("expert"), lax.axis_index("tensor")
    x, zl, y = e // (2 * NY), (e // NY) % 2, e % NY
    zh, c = t // 2, t % 2
    z = zh * 2 + zl
    group = ctx.shape[0]
    half = res.shape[1]
    blk = group // NHI
    other = 1 - c
    ffn = gw_h.shape[1]
    ways = (1, -1)

    def at_z(k):
        to = (z + k + NZ) % NZ
        return {"expert": (x * 2 + to % 2) * NY + y, "tensor": (to // 2) * 2 + c}

    def at_xy(i, sign):
        px = (x + sign * (i // NY) + NX) % NX
        py = (y + sign * (i % NY) + NY) % NY
        return {"expert": (px * 2 + zl) * NY + py, "tensor": t}

    core = {"expert": e, "tensor": zh * 2 + other}
    mate = {"expert": (x * 2 + (1 - zl)) * NY + y, "tensor": t}

    def place(k):
        to = (z + k + NZ) % NZ
        return (to % 2) * NHI + to // 2

    def send(src, dst, ss, rs, to):
        copy = pltpu.make_async_remote_copy(
            src_ref=src, dst_ref=dst, send_sem=ss, recv_sem=rs, device_id=to, device_id_type=MESH
        )
        copy.start()
        sent.append(copy)
        return copy

    sent = []

    loads = []

    def load(src, dst):
        copy = pltpu.make_async_copy(src, dst, load_sem.at[len(loads)])
        copy.start()
        loads.append(copy)
        return copy

    own_cols = pl.ds(pl.multiple_of(c * half, half), half)
    other_cols = pl.ds(pl.multiple_of(other * half, half), half)
    l_routes = load(routes_h, names.at[zl])
    l_gates = load(gates_h, gates.at[zl])
    l_ctx = load(ctx_h, ctx)
    l_ow1 = load(ow_h.at[:, other_cols], ow.at[0])
    l_ow0 = load(ow_h.at[:, own_cols], ow.at[1])
    l_res = load(res_h.at[pl.ds(pl.multiple_of(zh * blk, blk), blk), own_cols], res)
    l_gain = load(gain_h, gain)
    l_gw = load(gw_h, wgu.at[:, pl.ds(0, ffn)])
    l_uw = load(uw_h, wgu.at[:, pl.ds(ffn, ffn)])
    l_dw = load(dw_h, wd)

    barrier = pltpu.get_barrier_semaphore()

    def hello(i, carry):
        pl.semaphore_signal(barrier, inc=1, device_id=at_xy(i, 1), device_id_type=MESH)
        return carry

    lax.fori_loop(1, PEERS, hello, 0)
    for to in [at_z(k) for k in RING] + [core]:
        pl.semaphore_signal(barrier, inc=1, device_id=to, device_id_type=MESH)

    peer = lax.broadcasted_iota(jnp.int32, (PEERS, group), 0)
    px, py = (x + (peer >> 2)) & (NX - 1), (y + (peer & (NY - 1))) & (NY - 1)
    named = ((px * 2 + zl) * NY + py) * NHI + zh

    def slots_of(g, before):
        hit = jnp.zeros((PEERS, group), F32)
        weight = jnp.zeros((PEERS, group), F32)
        for k in range(names.shape[1]):
            same = names[g, k : k + 1, :] == named
            hit = hit + jnp.where(same, 1.0, 0.0)
            weight = weight + jnp.where(same, gates[g, k : k + 1, :], 0.0)
        earlier = (
            lax.broadcasted_iota(jnp.int32, (group, group), 0)
            < lax.broadcasted_iota(jnp.int32, (group, group), 1)
        ).astype(F32).astype(BF)
        rank = dot(hit.astype(BF), earlier) + before
        rank = jnp.where(hit > 0.0, rank, -1.0)
        slot = lax.broadcasted_iota(jnp.int32, (PEERS, SLOTS, group), 1).astype(F32)
        chosen = slot == rank[:, None, :]
        span = pl.ds(pl.multiple_of(g * group, group), group)
        pick[:, span] = jnp.where(chosen, 1.0, 0.0).reshape(ROWS, group).astype(BF)
        gated = jnp.where(chosen, jnp.broadcast_to(weight[:, None, :], chosen.shape), 0.0)
        spread[span, :] = gated.reshape(ROWS, group).T.astype(BF)
        return before + jnp.sum(hit, axis=1, keepdims=True)

    l_routes.wait()
    l_gates.wait()
    before = slots_of(zl, jnp.zeros((PEERS, 1), F32))

    l_ctx.wait()
    l_ow1.wait()
    for q, (k0, w) in enumerate(OUT):
        hp_send[:, k0 : k0 + w] = dot(ctx[...], ow[0, :, k0 : k0 + w]).astype(BF)
    l_ow0.wait()
    for q, (k0, w) in enumerate(OUT):
        total[:, k0 : k0 + w] = dot(ctx[...], ow[1, :, k0 : k0 + w])
    pl.semaphore_wait(barrier, PEERS + len(RING))
    hp_copies = []
    for q, (k0, w) in enumerate(OUT):
        cols = pl.ds(k0, w)
        hp_copies.append(send(hp_send.at[:, cols], hp_recv.at[:, cols], hp_ss.at[q], hp_rs.at[q], core))
    tables = [
        send(names.at[zl], names.at[zl], table_ss.at[0], table_rs.at[0], mate),
        send(gates.at[zl], gates.at[zl], table_ss.at[1], table_rs.at[1], mate),
    ]

    def rows_of(k):
        return pl.ds(pl.multiple_of(((zh + k + NHI) % NHI) * blk, blk), blk)

    relays, lasts = {}, {}

    def reduce_first(q):
        k0, w = OUT[q]
        cols = pl.ds(k0, w)
        way = ways[q % 2]
        hp_copies[q].wait_recv()
        total[:, cols] = total[:, cols] + hp_recv[:, cols].astype(F32)
        rs_send[0, :, cols] = total[rows_of(2), cols].astype(BF)
        relays[q] = send(rs_send.at[0, :, cols], rs_relay.at[:, cols], rs_ss.at[q, 0], relay_rs.at[q], at_z(2 * way))
        rs_send[1, :, cols] = total[rows_of(-way), cols].astype(BF)
        lasts[q, 1] = send(
            rs_send.at[1, :, cols], rs_last.at[1, :, cols], rs_ss.at[q, 1], last_rs.at[q, 1], at_z(-2 * way)
        )

    def reduce_second(q):
        k0, w = OUT[q]
        cols = pl.ds(k0, w)
        way = ways[q % 2]
        relays[q].wait_recv()
        rs_send[2, :, cols] = (total[rows_of(way), cols] + rs_relay[:, cols].astype(F32)).astype(BF)
        lasts[q, 0] = send(
            rs_send.at[2, :, cols], rs_last.at[0, :, cols], rs_ss.at[q, 2], last_rs.at[q, 0], at_z(2 * way)
        )

    for q in range(len(OUT)):
        reduce_first(q)

    for copy in tables:
        copy.wait_recv()
    slots_of(1 - zl, before)

    for q in range(len(OUT)):
        reduce_second(q)

    l_gain.wait()
    l_gw.wait()
    l_uw.wait()
    diagonal = lax.broadcasted_iota(jnp.int32, (128, 128), 0) == lax.broadcasted_iota(jnp.int32, (128, 128), 1)

    def fold(r, carry):
        column = jnp.sum(jnp.where(diagonal, gain[pl.ds(r, 1), :], 0.0), axis=1, keepdims=True)
        span = pl.ds(pl.multiple_of(r * 128, 128), 128)
        wgu[span, :] = (wgu[span, :].astype(F32) * column).astype(BF)
        return carry

    lax.fori_loop(0, gain.shape[0], fold, 0)
    l_res.wait()

    gathers = {}
    packs = {}

    def opposite(q, d):
        return q % 2 == d

    def to_peers(src, dst, ss, rs, q, cols, sign):
        def one(i, carry):
            span = pl.ds(i * SLABS, SLABS)
            pltpu.make_async_remote_copy(
                src_ref=src.at[span, :, cols],
                dst_ref=dst.at[span, :, cols],
                send_sem=ss.at[q], recv_sem=rs.at[q],
                device_id=at_xy(i, sign), device_id_type=MESH,
            ).start()
            return carry

        lax.fori_loop(1, PEERS, one, 0)
        rest = pl.ds(SLABS, (PEERS - 1) * SLABS)
        copy = pltpu.make_async_remote_copy(
            src_ref=src.at[rest, :, cols], dst_ref=dst.at[rest, :, cols],
            send_sem=ss.at[q], recv_sem=rs.at[q],
            device_id=at_xy(1, sign), device_id_type=MESH,
        )
        sent.append(copy)
        return copy

    def spread_own(q):
        k0, w = OUT[q]
        cols = pl.ds(k0, w)
        lasts[q, 1].wait_recv()
        lasts[q, 0].wait_recv()
        summed = total[rows_of(0), cols] + rs_last[0, :, cols].astype(F32) + rs_last[1, :, cols].astype(F32)
        toks[place(0), :, cols] = (res[:, cols].astype(F32) + summed).astype(BF)
        block = toks.at[place(0), :, cols]
        if q in OUT_DIRECT:
            at = OUT_DIRECT.index(q)
            for i in reversed(range(len(RING))):
                gathers[q, i] = send(block, block, all_ss.at[at, i], all_rs.at[at, i], at_z(RING[i]))
            return
        for n in (2, 1):
            for d, way in enumerate(ways):
                gathers[q, d, n] = send(
                    block, block, near_ss.at[q, d, n - 1], near_rs.at[q, d, n - 1], at_z(n * way)
                )

    def pass_on(q):
        if q in OUT_DIRECT:
            return
        k0, w = OUT[q]
        for d, way in enumerate(ways):
            gathers[q, d, 2].wait_recv()
            block = toks.at[place(-2 * way), :, pl.ds(k0, w)]
            for n in (2, 1) if opposite(q, d) else (1,):
                gathers[q, d, 2 + n] = send(
                    block, block, far_ss.at[q, d, n - 1], far_rs.at[q, d, n - 1], at_z(n * way)
                )

    def dispatch(q):
        k0, w = OUT[q]
        cols = pl.ds(k0, w)
        if q in OUT_DIRECT:
            for i in range(len(RING)):
                gathers[q, i].wait_recv()
        else:
            for d in range(2):
                for n in (1, 3, 4) if opposite(q, d) else (1, 3):
                    gathers[q, d, n].wait_recv()
        picked = dot(pick[...], toks[:, :, cols].reshape(2 * group, w)).astype(BF)
        picked = picked.reshape(PEERS * SLABS, 8, w)
        rows_own[0:SLABS, :, cols] = picked[0:SLABS]
        pack[SLABS:, :, cols] = picked[SLABS:]
        packs[q] = to_peers(pack, rows_own, pack_ss, pack_rs, q, cols, 1)

    spread_own(0)
    spread_own(1)
    for q in range(len(OUT)):
        pass_on(q)
        if q + 2 < len(OUT):
            spread_own(q + 2)
        if q:
            dispatch(q - 1)
    dispatch(len(OUT) - 1)

    def into(rows, q, side, first=False):
        k0, w = OUT[q]
        got = rows[:, :, k0 : k0 + w].reshape(ROWS, w)
        at = pl.multiple_of(side * half + k0, 128)
        product = dot(got, wgu[pl.ds(at, w), :])
        acc[...] = product if first else acc[...] + product
        wide = got.astype(F32)
        wide = wide * wide
        parts = [wide[:, n : n + 128] for n in range(0, w, 128)]
        if not first:
            parts.append(square[...])
        square[...] = functools.reduce(lambda a, b: a + b, parts)

    swaps = {}
    for q, (k0, w) in enumerate(OUT):
        packs[q].wait_recv()
        cols = pl.ds(k0, w)
        swaps[q] = send(rows_own.at[:, :, cols], rows_other.at[:, :, cols], swap_ss.at[q], swap_rs.at[q], core)
        into(rows_own, q, c, q == 0)
        if q:
            swaps[q - 1].wait_recv()
            into(rows_other, q - 1, other)
    swaps[len(OUT) - 1].wait_recv()
    into(rows_other, len(OUT) - 1, other)
    l_dw.wait()

    mean = jnp.sum(square[...], axis=1, keepdims=True) / (2 * half)
    inverse = lax.rsqrt(mean + 1e-06)
    gate = acc[:, 0:ffn] * inverse
    act[...] = (gate / (1.0 + jnp.exp(-gate)) * (acc[:, ffn : 2 * ffn] * inverse)).astype(BF)

    crossing, backs = {}, {}

    def out_of(q, side):
        k0, w = BACK[q]
        return dot(act[...], wd[:, pl.ds(pl.multiple_of(side * half + k0, 128), w)])

    def cross(q):
        k0, w = BACK[q]
        cols = pl.ds(k0, w)
        y_send[:, cols] = out_of(q, other).astype(BF)
        crossing[q] = send(y_send.at[:, cols], y_recv.at[:, cols], y_ss.at[q], y_rs.at[q], core)

    cross(0)
    for q, (k0, w) in enumerate(BACK):
        if q + 1 < len(BACK):
            cross(q + 1)
        cols = pl.ds(k0, w)
        own = out_of(q, c)
        crossing[q].wait_recv()
        both = (own + y_recv[:, cols].astype(F32)).astype(BF).reshape(PEERS * SLABS, 8, w)
        ret[0:SLABS, :, cols] = both[0:SLABS]
        back[SLABS:, :, cols] = both[SLABS:]
        backs[q] = to_peers(back, ret, back_ss, back_rs, q, cols, -1)

    sums = {}

    def combine(q):
        k0, w = BACK[q]
        cols = pl.ds(k0, w)
        backs[q].wait_recv()
        part[:, :, cols] = dot(spread[...], ret[:, :, cols].reshape(ROWS, w)).reshape(NZ, blk, w)
        if q in BACK_DIRECT:
            at = BACK_DIRECT.index(q)
            for i in reversed(range(len(RING))):
                all_send[i, :, cols] = part[place(RING[i]), :, cols].astype(BF)
                sums[q, i] = send(
                    all_send.at[i, :, cols], all_recv.at[i, :, cols],
                    allsum_ss.at[at, i], allsum_rs.at[at, i], at_z(RING[i]),
                )
            return
        for d, way in enumerate(ways):
            for n in (2, 1) if opposite(q, d) else (1,):
                far_send[d, n - 1, :, cols] = part[place((2 + n) * way), :, cols].astype(BF)
                sums[q, d, 2 + n] = send(
                    far_send.at[d, n - 1, :, cols], far_recv.at[d, n - 1, :, cols],
                    farsum_ss.at[q, d, n - 1], farsum_rs.at[q, d, n - 1], at_z(n * way),
                )
        for d, way in enumerate(ways):
            near_send[d, 0, :, cols] = part[place(way), :, cols].astype(BF)
            sums[q, d, 1] = send(
                near_send.at[d, 0, :, cols], near_recv.at[d, 0, :, cols],
                nearsum_ss.at[q, d, 0], nearsum_rs.at[q, d, 0], at_z(way),
            )

    def add_on(q):
        if q in BACK_DIRECT:
            return
        k0, w = BACK[q]
        cols = pl.ds(k0, w)
        for d, way in enumerate(ways):
            value = part[place(2 * way), :, cols]
            for n in (2, 1) if opposite(q, d) else (1,):
                sums[q, d, 2 + n].wait_recv()
                value = value + far_recv[d, n - 1, :, cols].astype(F32)
            near_send[d, 1, :, cols] = value.astype(BF)
            sums[q, d, 2] = send(
                near_send.at[d, 1, :, cols], near_recv.at[d, 1, :, cols],
                nearsum_ss.at[q, d, 1], nearsum_rs.at[q, d, 1], at_z(2 * way),
            )

    def finish(q):
        k0, w = BACK[q]
        cols = pl.ds(k0, w)
        value = part[place(0), :, cols]
        if q in BACK_DIRECT:
            for i in range(len(RING)):
                sums[q, i].wait_recv()
                value = value + all_recv[i, :, cols].astype(F32)
        else:
            for d in range(2):
                for n in (1, 2):
                    sums[q, d, n].wait_recv()
                    value = value + near_recv[d, n - 1, :, cols].astype(F32)
        fin[:, cols] = (toks[place(0), :, cols].astype(F32) + value).astype(BF)

    for q in range(len(BACK)):
        combine(q)
        if q:
            add_on(q - 1)
    add_on(len(BACK) - 1)
    for q in range(len(BACK)):
        finish(q)

    few = blk // 2
    keep = pl.ds(pl.multiple_of(c * few, few), few)
    give = pl.ds(pl.multiple_of(other * few, few), few)
    fin_send[...] = fin[give, :]
    last = send(fin_send, fin_recv, fin_ss, fin_rs, core)
    out_ref[:, own_cols] = fin[keep, :]
    last.wait_recv()
    out_ref[:, other_cols] = fin_recv[...]
    for copy in sent:
        copy.wait_send()


def local(context, output_weight, residual, norm_gain, routes, gate_values, gate_weight, up_weight, down_weight):
    group, heads = context.shape
    width = residual.shape[1]
    half = width // 2
    blk = group // NHI
    ffn = gate_weight.shape[1]
    topk = routes.shape[1]
    dma = pltpu.SemaphoreType.DMA
    vm = pltpu.VMEM
    q, p = len(OUT), len(BACK)
    slabs = PEERS * SLABS
    scratch = [
        vm((group, heads), BF), vm((2, heads, half), BF), vm((blk, half), BF), vm((width // 128, 128), F32),
        vm((width, 2 * ffn), BF), vm((ffn, width), BF), dma((10,)),
        vm((group, half), BF), vm((group, half), BF), dma((q,)), dma((q,)), vm((group, half), F32),
        vm((3, blk, half), BF), vm((blk, half), BF), vm((2, blk, half), BF), dma((q, 3)), dma((q,)), dma((q, 2)),
        vm((2, topk, group), jnp.int32), vm((2, topk, group), F32), dma((2,)), dma((2,)),
        vm((ROWS, 2 * group), BF), vm((2 * group, ROWS), BF),
        vm((NZ, blk, half), BF), dma((q, 2, 2)), dma((q, 2, 2)), dma((q, 2, 2)), dma((q, 2, 2)),
        dma((len(OUT_DIRECT), len(RING))), dma((len(OUT_DIRECT), len(RING))),
        vm((slabs, 8, half), BF), vm((slabs, 8, half), BF), vm((slabs, 8, half), BF),
        dma((q,)), dma((q,)), dma((q,)), dma((q,)),
        vm((ROWS, 2 * ffn), F32), vm((ROWS, 128), F32), vm((ROWS, ffn), BF),
        vm((ROWS, half), BF), vm((ROWS, half), BF), dma((p,)), dma((p,)),
        vm((slabs, 8, half), BF), vm((slabs, 8, half), BF), dma((p,)), dma((p,)),
        vm((NZ, blk, half), F32),
        vm((2, 2, blk, half), BF), vm((2, 2, blk, half), BF), dma((p, 2, 2)), dma((p, 2, 2)),
        vm((2, 2, blk, half), BF), vm((2, 2, blk, half), BF), dma((p, 2, 2)), dma((p, 2, 2)),
        vm((len(RING), blk, half), BF), vm((len(RING), blk, half), BF),
        dma((len(BACK_DIRECT), len(RING))), dma((len(BACK_DIRECT), len(RING))),
        vm((blk, half), BF), vm((blk // 2, half), BF), vm((blk // 2, half), BF), dma(()), dma(()),
    ]
    return pl.pallas_call(
        kernel,
        out_shape=jax.ShapeDtypeStruct((blk // 2, width), BF),
        in_specs=[pl.BlockSpec(memory_space=pl.ANY)] * 9,
        out_specs=pl.BlockSpec(memory_space=pltpu.VMEM),
        scratch_shapes=scratch,
        compiler_params=pltpu.CompilerParams(
            collective_id=0, has_side_effects=True, vmem_limit_bytes=56 * 2**20
        ),
        cost_estimate=pl.CostEstimate(flops=4 * 10**9, bytes_accessed=10**7, transcendentals=0),
    )(context, output_weight, residual, norm_gain.reshape(-1, 128), routes.T, gate_values.T, gate_weight, up_weight, down_weight)


def solution(mesh):
    in_specs = (
        P("expert", "tensor"),
        P("tensor", None),
        P("expert", None),
        P(),
        P("expert", None),
        P("expert", None),
        P(None, ("expert", "tensor")),
        P(None, ("expert", "tensor")),
        P(("expert", "tensor"), None),
    )
    out_specs = P(("expert", "tensor"), None)
    return jax.shard_map(local, mesh=mesh, in_specs=in_specs, out_specs=out_specs, check_vma=False)
```

```python
import functools

import jax
import jax.numpy as jnp
from jax import lax
from jax.experimental import pallas as pl
from jax.experimental.pallas import tpu as pltpu
from jax.sharding import PartitionSpec as P

MESH = pl.DeviceIdType.MESH
NX, NY, NZ, NHI = 4, 4, 8, 4
PEERS = NX * NY
SLABS = 5
SLOTS = SLABS * 8
ROWS = PEERS * SLOTS
OUT = ((0, 128), (128, 256), (384, 256), (640, 256), (896, 128))
BACK = ((0, 256), (256, 256), (512, 256), (768, 128), (896, 128))
OUT_STEPS = (2, 2, 2, 2, 2)
BACK_STEPS = (3, 3, 3, 2, 1)
OUT_DIRECT = [q for q, n in enumerate(OUT_STEPS) if n == 1]
BACK_DIRECT = [q for q, n in enumerate(BACK_STEPS) if n == 1]
RING = (1, -1, 2, -2, 3, -3, 4)
BF, F32 = jnp.bfloat16, jnp.float32


def dot(a, b):
    return jnp.dot(a, b, preferred_element_type=F32)


def kernel(
    ctx_h, ow_h, res_h, gain_h, routes_h, gates_h, gw_h, uw_h, dw_h, out_ref,
    ctx, ow, res, gain, wgu, wd, load_sem,
    hp_send, hp_recv, hp_ss, hp_rs, total,
    rs_send, rs_relay, rs_last, rs_ss, relay_rs, last_rs,
    names, gates, table_ss, table_rs, pick, spread,
    toks, near_ss, near_rs, far_ss, far_rs, all_ss, all_rs,
    pack, rows_own, rows_other, pack_ss, pack_rs, swap_ss, swap_rs,
    acc, square, act, y_send, y_recv, y_ss, y_rs,
    back, ret, back_ss, back_rs,
    part, far_send, far_recv, farsum_ss, farsum_rs, near_send, near_recv, nearsum_ss, nearsum_rs,
    all_send, all_recv, allsum_ss, allsum_rs,
    fin, fin_send, fin_recv, fin_ss, fin_rs,
):
    e, t = lax.axis_index("expert"), lax.axis_index("tensor")
    x, zl, y = e // (2 * NY), (e // NY) % 2, e % NY
    zh, c = t // 2, t % 2
    z = zh * 2 + zl
    group = ctx.shape[0]
    half = res.shape[1]
    blk = group // NHI
    other = 1 - c
    ffn = gw_h.shape[1]
    ways = (1, -1)

    def at_z(k):
        to = (z + k + NZ) % NZ
        return {"expert": (x * 2 + to % 2) * NY + y, "tensor": (to // 2) * 2 + c}

    def at_xy(i, sign):
        px = (x + sign * (i // NY) + NX) % NX
        py = (y + sign * (i % NY) + NY) % NY
        return {"expert": (px * 2 + zl) * NY + py, "tensor": t}

    core = {"expert": e, "tensor": zh * 2 + other}
    mate = {"expert": (x * 2 + (1 - zl)) * NY + y, "tensor": t}

    def place(k):
        to = (z + k + NZ) % NZ
        return (to % 2) * NHI + to // 2

    def send(src, dst, ss, rs, to):
        copy = pltpu.make_async_remote_copy(
            src_ref=src, dst_ref=dst, send_sem=ss, recv_sem=rs, device_id=to, device_id_type=MESH
        )
        copy.start()
        sent.append(copy)
        return copy

    sent = []

    loads = []

    def load(src, dst):
        copy = pltpu.make_async_copy(src, dst, load_sem.at[len(loads)])
        copy.start()
        loads.append(copy)
        return copy

    own_cols = pl.ds(pl.multiple_of(c * half, half), half)
    other_cols = pl.ds(pl.multiple_of(other * half, half), half)
    l_routes = load(routes_h, names.at[zl])
    l_gates = load(gates_h, gates.at[zl])
    l_ctx = load(ctx_h, ctx)
    l_ow1 = load(ow_h.at[:, other_cols], ow.at[0])
    l_ow0 = load(ow_h.at[:, own_cols], ow.at[1])
    l_res = load(res_h.at[pl.ds(pl.multiple_of(zh * blk, blk), blk), own_cols], res)
    l_gain = load(gain_h, gain)
    l_gw = load(gw_h, wgu.at[:, pl.ds(0, ffn)])
    l_uw = load(uw_h, wgu.at[:, pl.ds(ffn, ffn)])
    l_dw = load(dw_h, wd)

    barrier = pltpu.get_barrier_semaphore()

    def hello(i, carry):
        pl.semaphore_signal(barrier, inc=1, device_id=at_xy(i, 1), device_id_type=MESH)
        return carry

    lax.fori_loop(1, PEERS, hello, 0)
    for to in [at_z(k) for k in RING] + [core]:
        pl.semaphore_signal(barrier, inc=1, device_id=to, device_id_type=MESH)

    peer = lax.broadcasted_iota(jnp.int32, (PEERS, group), 0)
    px, py = (x + (peer >> 2)) & (NX - 1), (y + (peer & (NY - 1))) & (NY - 1)
    named = ((px * 2 + zl) * NY + py) * NHI + zh

    def slots_of(g, before):
        hit = jnp.zeros((PEERS, group), F32)
        weight = jnp.zeros((PEERS, group), F32)
        for k in range(names.shape[1]):
            same = names[g, k : k + 1, :] == named
            hit = hit + jnp.where(same, 1.0, 0.0)
            weight = weight + jnp.where(same, gates[g, k : k + 1, :], 0.0)
        earlier = (
            lax.broadcasted_iota(jnp.int32, (group, group), 0)
            < lax.broadcasted_iota(jnp.int32, (group, group), 1)
        ).astype(F32).astype(BF)
        rank = dot(hit.astype(BF), earlier) + before
        rank = jnp.where(hit > 0.0, rank, -1.0)
        slot = lax.broadcasted_iota(jnp.int32, (PEERS, SLOTS, group), 1).astype(F32)
        chosen = slot == rank[:, None, :]
        span = pl.ds(pl.multiple_of(g * group, group), group)
        pick[:, span] = jnp.where(chosen, 1.0, 0.0).reshape(ROWS, group).astype(BF)
        gated = jnp.where(chosen, jnp.broadcast_to(weight[:, None, :], chosen.shape), 0.0)
        spread[span, :] = gated.reshape(ROWS, group).T.astype(BF)
        return before + jnp.sum(hit, axis=1, keepdims=True)

    l_routes.wait()
    l_gates.wait()
    before = slots_of(zl, jnp.zeros((PEERS, 1), F32))

    l_ctx.wait()
    l_ow1.wait()
    for q, (k0, w) in enumerate(OUT):
        hp_send[:, k0 : k0 + w] = dot(ctx[...], ow[0, :, k0 : k0 + w]).astype(BF)
    l_ow0.wait()
    for q, (k0, w) in enumerate(OUT):
        total[:, k0 : k0 + w] = dot(ctx[...], ow[1, :, k0 : k0 + w])
    pl.semaphore_wait(barrier, PEERS + len(RING))
    hp_copies = []
    for q, (k0, w) in enumerate(OUT):
        cols = pl.ds(k0, w)
        hp_copies.append(send(hp_send.at[:, cols], hp_recv.at[:, cols], hp_ss.at[q], hp_rs.at[q], core))
    tables = [
        send(names.at[zl], names.at[zl], table_ss.at[0], table_rs.at[0], mate),
        send(gates.at[zl], gates.at[zl], table_ss.at[1], table_rs.at[1], mate),
    ]

    def rows_of(k):
        return pl.ds(pl.multiple_of(((zh + k + NHI) % NHI) * blk, blk), blk)

    relays, lasts = {}, {}

    def reduce_first(q):
        k0, w = OUT[q]
        cols = pl.ds(k0, w)
        way = ways[q % 2]
        hp_copies[q].wait_recv()
        total[:, cols] = total[:, cols] + hp_recv[:, cols].astype(F32)
        rs_send[0, :, cols] = total[rows_of(2), cols].astype(BF)
        relays[q] = send(rs_send.at[0, :, cols], rs_relay.at[:, cols], rs_ss.at[q, 0], relay_rs.at[q], at_z(2 * way))

    def reduce_direct(q):
        k0, w = OUT[q]
        cols = pl.ds(k0, w)
        way = ways[q % 2]
        rs_send[1, :, cols] = total[rows_of(-way), cols].astype(BF)
        lasts[q, 1] = send(
            rs_send.at[1, :, cols], rs_last.at[1, :, cols], rs_ss.at[q, 1], last_rs.at[q, 1], at_z(-2 * way)
        )

    def reduce_second(q):
        k0, w = OUT[q]
        cols = pl.ds(k0, w)
        way = ways[q % 2]
        relays[q].wait_recv()
        rs_send[2, :, cols] = (total[rows_of(way), cols] + rs_relay[:, cols].astype(F32)).astype(BF)
        lasts[q, 0] = send(
            rs_send.at[2, :, cols], rs_last.at[0, :, cols], rs_ss.at[q, 2], last_rs.at[q, 0], at_z(2 * way)
        )

    for q in range(len(OUT)):
        reduce_first(q)
    for q in range(len(OUT)):
        reduce_direct(q)

    for copy in tables:
        copy.wait_recv()
    slots_of(1 - zl, before)

    l_gain.wait()
    l_gw.wait()
    l_uw.wait()
    diagonal = lax.broadcasted_iota(jnp.int32, (128, 128), 0) == lax.broadcasted_iota(jnp.int32, (128, 128), 1)

    def fold(r, carry):
        column = jnp.sum(jnp.where(diagonal, gain[pl.ds(r, 1), :], 0.0), axis=1, keepdims=True)
        span = pl.ds(pl.multiple_of(r * 128, 128), 128)
        wgu[span, :] = (wgu[span, :].astype(F32) * column).astype(BF)
        return carry

    lax.fori_loop(0, gain.shape[0], fold, 0)
    for q in range(len(OUT)):
        reduce_second(q)

    l_res.wait()

    gathers = {}
    packs = {}

    def in_order(stages, count, steps):
        todo = []
        for q in range(count):
            lags = {1: (0, 0, 0, 1.1), 2: (0, 1.1, 1.1, 2.2), 3: (0, 1.1, 2.2, 3.3)}[steps[q]]
            todo += [(q + lag, q, n) for n, lag in enumerate(lags)]
        for _, q, n in sorted(todo, key=lambda item: (item[0], item[2])):
            stages[n](q)

    def opposite(q, d):
        return q % 2 == d

    def to_peers(src, dst, ss, rs, q, cols, sign):
        def one(i, carry):
            span = pl.ds(i * SLABS, SLABS)
            pltpu.make_async_remote_copy(
                src_ref=src.at[span, :, cols],
                dst_ref=dst.at[span, :, cols],
                send_sem=ss.at[q], recv_sem=rs.at[q],
                device_id=at_xy(i, sign), device_id_type=MESH,
            ).start()
            return carry

        lax.fori_loop(1, PEERS, one, 0)
        rest = pl.ds(SLABS, (PEERS - 1) * SLABS)
        copy = pltpu.make_async_remote_copy(
            src_ref=src.at[rest, :, cols], dst_ref=dst.at[rest, :, cols],
            send_sem=ss.at[q], recv_sem=rs.at[q],
            device_id=at_xy(1, sign), device_id_type=MESH,
        )
        sent.append(copy)
        return copy

    def spread_own(q):
        k0, w = OUT[q]
        cols = pl.ds(k0, w)
        lasts[q, 1].wait_recv()
        lasts[q, 0].wait_recv()
        summed = total[rows_of(0), cols] + rs_last[0, :, cols].astype(F32) + rs_last[1, :, cols].astype(F32)
        toks[place(0), :, cols] = (res[:, cols].astype(F32) + summed).astype(BF)
        block = toks.at[place(0), :, cols]
        if q in OUT_DIRECT:
            at = OUT_DIRECT.index(q)
            for i in reversed(range(len(RING))):
                gathers[q, i] = send(block, block, all_ss.at[at, i], all_rs.at[at, i], at_z(RING[i]))
            return
        for n in (2, 1) if OUT_STEPS[q] == 2 else (1,):
            for d, way in enumerate(ways):
                gathers[q, d, n] = send(
                    block, block, near_ss.at[q, d, n - 1], near_rs.at[q, d, n - 1], at_z(n * way)
                )

    def pass_near(q):
        if OUT_STEPS[q] != 3:
            return
        k0, w = OUT[q]
        for d, way in enumerate(ways):
            gathers[q, d, 1].wait_recv()
            block = toks.at[place(-way), :, pl.ds(k0, w)]
            gathers[q, d, 2] = send(block, block, near_ss.at[q, d, 1], near_rs.at[q, d, 1], at_z(way))

    def pass_on(q):
        if q in OUT_DIRECT:
            return
        k0, w = OUT[q]
        for d, way in enumerate(ways):
            gathers[q, d, 2].wait_recv()
            block = toks.at[place(-2 * way), :, pl.ds(k0, w)]
            for n in (2, 1) if opposite(q, d) else (1,):
                gathers[q, d, 2 + n] = send(
                    block, block, far_ss.at[q, d, n - 1], far_rs.at[q, d, n - 1], at_z(n * way)
                )

    def dispatch(q):
        k0, w = OUT[q]
        cols = pl.ds(k0, w)
        if q in OUT_DIRECT:
            for i in range(len(RING)):
                gathers[q, i].wait_recv()
        else:
            for d in range(2):
                if OUT_STEPS[q] == 2:
                    gathers[q, d, 1].wait_recv()
                for n in (3, 4) if opposite(q, d) else (3,):
                    gathers[q, d, n].wait_recv()
        picked = dot(pick[...], toks[:, :, cols].reshape(2 * group, w)).astype(BF)
        picked = picked.reshape(PEERS * SLABS, 8, w)
        rows_own[0:SLABS, :, cols] = picked[0:SLABS]
        pack[SLABS:, :, cols] = picked[SLABS:]
        packs[q] = to_peers(pack, rows_own, pack_ss, pack_rs, q, cols, 1)

    in_order((spread_own, pass_near, pass_on, dispatch), len(OUT), OUT_STEPS)

    def into(rows, q, side, first=False):
        k0, w = OUT[q]
        got = rows[:, :, k0 : k0 + w].reshape(ROWS, w)
        at = pl.multiple_of(side * half + k0, 128)
        product = dot(got, wgu[pl.ds(at, w), :])
        acc[...] = product if first else acc[...] + product
        wide = got.astype(F32)
        wide = wide * wide
        parts = [wide[:, n : n + 128] for n in range(0, w, 128)]
        if not first:
            parts.append(square[...])
        square[...] = functools.reduce(lambda a, b: a + b, parts)

    swaps = {}
    for q, (k0, w) in enumerate(OUT):
        packs[q].wait_recv()
        cols = pl.ds(k0, w)
        swaps[q] = send(rows_own.at[:, :, cols], rows_other.at[:, :, cols], swap_ss.at[q], swap_rs.at[q], core)
        into(rows_own, q, c, q == 0)
        if q:
            swaps[q - 1].wait_recv()
            into(rows_other, q - 1, other)
    swaps[len(OUT) - 1].wait_recv()
    into(rows_other, len(OUT) - 1, other)
    l_dw.wait()

    mean = jnp.sum(square[...], axis=1, keepdims=True) / (2 * half)
    inverse = lax.rsqrt(mean + 1e-06)
    gate = acc[:, 0:ffn] * inverse
    act[...] = (gate / (1.0 + jnp.exp(-gate)) * (acc[:, ffn : 2 * ffn] * inverse)).astype(BF)

    crossing, backs = {}, {}

    def out_of(q, side):
        k0, w = BACK[q]
        return dot(act[...], wd[:, pl.ds(pl.multiple_of(side * half + k0, 128), w)])

    def cross(q):
        k0, w = BACK[q]
        cols = pl.ds(k0, w)
        y_send[:, cols] = out_of(q, other).astype(BF)
        crossing[q] = send(y_send.at[:, cols], y_recv.at[:, cols], y_ss.at[q], y_rs.at[q], core)

    cross(0)
    for q, (k0, w) in enumerate(BACK):
        if q + 1 < len(BACK):
            cross(q + 1)
        cols = pl.ds(k0, w)
        own = out_of(q, c)
        crossing[q].wait_recv()
        both = (own + y_recv[:, cols].astype(F32)).astype(BF).reshape(PEERS * SLABS, 8, w)
        ret[0:SLABS, :, cols] = both[0:SLABS]
        back[SLABS:, :, cols] = both[SLABS:]
        backs[q] = to_peers(back, ret, back_ss, back_rs, q, cols, -1)

    sums = {}

    def combine(q):
        k0, w = BACK[q]
        cols = pl.ds(k0, w)
        backs[q].wait_recv()
        part[:, :, cols] = dot(spread[...], ret[:, :, cols].reshape(ROWS, w)).reshape(NZ, blk, w)
        if q in BACK_DIRECT:
            at = BACK_DIRECT.index(q)
            for i in reversed(range(len(RING))):
                all_send[i, :, cols] = part[place(RING[i]), :, cols].astype(BF)
                sums[q, i] = send(
                    all_send.at[i, :, cols], all_recv.at[i, :, cols],
                    allsum_ss.at[at, i], allsum_rs.at[at, i], at_z(RING[i]),
                )
            return
        for d, way in enumerate(ways):
            for n in (2, 1) if opposite(q, d) else (1,):
                far_send[d, n - 1, :, cols] = part[place((2 + n) * way), :, cols].astype(BF)
                sums[q, d, 2 + n] = send(
                    far_send.at[d, n - 1, :, cols], far_recv.at[d, n - 1, :, cols],
                    farsum_ss.at[q, d, n - 1], farsum_rs.at[q, d, n - 1], at_z(n * way),
                )
        for d, way in enumerate(ways) if BACK_STEPS[q] == 2 else ():
            near_send[d, 0, :, cols] = part[place(way), :, cols].astype(BF)
            sums[q, d, 1] = send(
                near_send.at[d, 0, :, cols], near_recv.at[d, 0, :, cols],
                nearsum_ss.at[q, d, 0], nearsum_rs.at[q, d, 0], at_z(way),
            )

    def add_on(q):
        if q in BACK_DIRECT:
            return
        far = 1 if BACK_STEPS[q] == 3 else 2
        k0, w = BACK[q]
        cols = pl.ds(k0, w)
        for d, way in enumerate(ways):
            value = part[place(2 * way), :, cols]
            for n in (2, 1) if opposite(q, d) else (1,):
                sums[q, d, 2 + n].wait_recv()
                value = value + far_recv[d, n - 1, :, cols].astype(F32)
            near_send[d, 1, :, cols] = value.astype(BF)
            sums[q, d, 2] = send(
                near_send.at[d, 1, :, cols], near_recv.at[d, 1, :, cols],
                nearsum_ss.at[q, d, 1], nearsum_rs.at[q, d, 1], at_z(far * way),
            )

    def add_near(q):
        if BACK_STEPS[q] != 3:
            return
        k0, w = BACK[q]
        cols = pl.ds(k0, w)
        for d, way in enumerate(ways):
            sums[q, d, 2].wait_recv()
            value = part[place(way), :, cols] + near_recv[d, 1, :, cols].astype(F32)
            near_send[d, 0, :, cols] = value.astype(BF)
            sums[q, d, 1] = send(
                near_send.at[d, 0, :, cols], near_recv.at[d, 0, :, cols],
                nearsum_ss.at[q, d, 0], nearsum_rs.at[q, d, 0], at_z(way),
            )

    def finish(q):
        k0, w = BACK[q]
        cols = pl.ds(k0, w)
        value = part[place(0), :, cols]
        if q in BACK_DIRECT:
            for i in range(len(RING)):
                sums[q, i].wait_recv()
                value = value + all_recv[i, :, cols].astype(F32)
        else:
            for d in range(2):
                for n in (1, 2) if BACK_STEPS[q] == 2 else (1,):
                    sums[q, d, n].wait_recv()
                    value = value + near_recv[d, n - 1, :, cols].astype(F32)
        fin[:, cols] = (toks[place(0), :, cols].astype(F32) + value).astype(BF)

    in_order((combine, add_on, add_near, finish), len(BACK), BACK_STEPS)

    few = blk // 2
    keep = pl.ds(pl.multiple_of(c * few, few), few)
    give = pl.ds(pl.multiple_of(other * few, few), few)
    fin_send[...] = fin[give, :]
    last = send(fin_send, fin_recv, fin_ss, fin_rs, core)
    out_ref[:, own_cols] = fin[keep, :]
    last.wait_recv()
    out_ref[:, other_cols] = fin_recv[...]
    for copy in sent:
        copy.wait_send()


def local(context, output_weight, residual, norm_gain, routes, gate_values, gate_weight, up_weight, down_weight):
    group, heads = context.shape
    width = residual.shape[1]
    half = width // 2
    blk = group // NHI
    ffn = gate_weight.shape[1]
    topk = routes.shape[1]
    dma = pltpu.SemaphoreType.DMA
    vm = pltpu.VMEM
    q, p = len(OUT), len(BACK)
    slabs = PEERS * SLABS
    scratch = [
        vm((group, heads), BF), vm((2, heads, half), BF), vm((blk, half), BF), vm((width // 128, 128), F32),
        vm((width, 2 * ffn), BF), vm((ffn, width), BF), dma((10,)),
        vm((group, half), BF), vm((group, half), BF), dma((q,)), dma((q,)), vm((group, half), F32),
        vm((3, blk, half), BF), vm((blk, half), BF), vm((2, blk, half), BF), dma((q, 3)), dma((q,)), dma((q, 2)),
        vm((2, topk, group), jnp.int32), vm((2, topk, group), F32), dma((2,)), dma((2,)),
        vm((ROWS, 2 * group), BF), vm((2 * group, ROWS), BF),
        vm((NZ, blk, half), BF), dma((q, 2, 2)), dma((q, 2, 2)), dma((q, 2, 2)), dma((q, 2, 2)),
        dma((max(1, len(OUT_DIRECT)), len(RING))), dma((max(1, len(OUT_DIRECT)), len(RING))),
        vm((slabs, 8, half), BF), vm((slabs, 8, half), BF), vm((slabs, 8, half), BF),
        dma((q,)), dma((q,)), dma((q,)), dma((q,)),
        vm((ROWS, 2 * ffn), F32), vm((ROWS, 128), F32), vm((ROWS, ffn), BF),
        vm((ROWS, half), BF), vm((ROWS, half), BF), dma((p,)), dma((p,)),
        vm((slabs, 8, half), BF), vm((slabs, 8, half), BF), dma((p,)), dma((p,)),
        vm((NZ, blk, half), F32),
        vm((2, 2, blk, half), BF), vm((2, 2, blk, half), BF), dma((p, 2, 2)), dma((p, 2, 2)),
        vm((2, 2, blk, half), BF), vm((2, 2, blk, half), BF), dma((p, 2, 2)), dma((p, 2, 2)),
        vm((len(RING), blk, half), BF), vm((len(RING), blk, half), BF),
        dma((max(1, len(BACK_DIRECT)), len(RING))), dma((max(1, len(BACK_DIRECT)), len(RING))),
        vm((blk, half), BF), vm((blk // 2, half), BF), vm((blk // 2, half), BF), dma(()), dma(()),
    ]
    return pl.pallas_call(
        kernel,
        out_shape=jax.ShapeDtypeStruct((blk // 2, width), BF),
        in_specs=[pl.BlockSpec(memory_space=pl.ANY)] * 9,
        out_specs=pl.BlockSpec(memory_space=pltpu.VMEM),
        scratch_shapes=scratch,
        compiler_params=pltpu.CompilerParams(
            collective_id=0, has_side_effects=True, vmem_limit_bytes=56 * 2**20
        ),
        cost_estimate=pl.CostEstimate(flops=4 * 10**9, bytes_accessed=10**7, transcendentals=0),
    )(context, output_weight, residual, norm_gain.reshape(-1, 128), routes.T, gate_values.T, gate_weight, up_weight, down_weight)


def solution(mesh):
    in_specs = (
        P("expert", "tensor"),
        P("tensor", None),
        P("expert", None),
        P(),
        P("expert", None),
        P("expert", None),
        P(None, ("expert", "tensor")),
        P(None, ("expert", "tensor")),
        P(("expert", "tensor"), None),
    )
    out_specs = P(("expert", "tensor"), None)
    return jax.shard_map(local, mesh=mesh, in_specs=in_specs, out_specs=out_specs, check_vma=False)
```

```python
import functools

import jax
import jax.numpy as jnp
from jax import lax
from jax.experimental import pallas as pl
from jax.experimental.pallas import tpu as pltpu
from jax.sharding import PartitionSpec as P

MESH = pl.DeviceIdType.MESH
NX, NY, NZ, NHI = 4, 4, 8, 4
PEERS = NX * NY
SLABS = 5
SLOTS = SLABS * 8
ROWS = PEERS * SLOTS
OUT = ((0, 128), (128, 256), (384, 256), (640, 256), (896, 128))
BACK = ((0, 128), (128, 256), (384, 256), (640, 256), (896, 128))
OUT_STEPS = (2, 2, 2, 2, 2)
BACK_STEPS = (3, 3, 3, 2, 1)
OUT_DIRECT = [q for q, n in enumerate(OUT_STEPS) if n == 1]
BACK_DIRECT = [q for q, n in enumerate(BACK_STEPS) if n == 1]
RING = (1, -1, 2, -2, 3, -3, 4)
BF, F32 = jnp.bfloat16, jnp.float32


def dot(a, b):
    return jnp.dot(a, b, preferred_element_type=F32)


def kernel(
    ctx_h, ow_h, res_h, gain_h, routes_h, gates_h, gw_h, uw_h, dw_h, out_ref,
    ctx, ow, res, gain, wgu, wd, load_sem,
    hp_send, hp_recv, hp_ss, hp_rs, total,
    rs_send, rs_relay, rs_last, rs_ss, relay_rs, last_rs,
    names, gates, table_ss, table_rs, pick, spread,
    toks, near_ss, near_rs, far_ss, far_rs, all_ss, all_rs,
    pack, rows_own, rows_other, pack_ss, pack_rs, swap_ss, swap_rs,
    acc, square, act, y_send, y_recv, y_ss, y_rs,
    back, ret, back_ss, back_rs,
    part, far_send, far_recv, farsum_ss, farsum_rs, near_send, near_recv, nearsum_ss, nearsum_rs,
    all_send, all_recv, allsum_ss, allsum_rs,
    fin, fin_send, fin_recv, fin_ss, fin_rs,
):
    e, t = lax.axis_index("expert"), lax.axis_index("tensor")
    x, zl, y = e // (2 * NY), (e // NY) % 2, e % NY
    zh, c = t // 2, t % 2
    z = zh * 2 + zl
    group = ctx.shape[0]
    half = res.shape[1]
    blk = group // NHI
    other = 1 - c
    ffn = gw_h.shape[1]
    ways = (1, -1)

    def at_z(k):
        to = (z + k + NZ) % NZ
        return {"expert": (x * 2 + to % 2) * NY + y, "tensor": (to // 2) * 2 + c}

    def at_xy(i, sign):
        px = (x + sign * (i // NY) + NX) % NX
        py = (y + sign * (i % NY) + NY) % NY
        return {"expert": (px * 2 + zl) * NY + py, "tensor": t}

    core = {"expert": e, "tensor": zh * 2 + other}
    mate = {"expert": (x * 2 + (1 - zl)) * NY + y, "tensor": t}

    def place(k):
        to = (z + k + NZ) % NZ
        return (to % 2) * NHI + to // 2

    def send(src, dst, ss, rs, to):
        copy = pltpu.make_async_remote_copy(
            src_ref=src, dst_ref=dst, send_sem=ss, recv_sem=rs, device_id=to, device_id_type=MESH
        )
        copy.start()
        sent.append(copy)
        return copy

    sent = []

    barrier = pltpu.get_barrier_semaphore()
    for to in [at_xy(i, 1) for i in range(PEERS - 1, 0, -1)] + [at_z(k) for k in reversed(RING)] + [core]:
        pl.semaphore_signal(barrier, inc=1, device_id=to, device_id_type=MESH)
    loads = []

    def load(src, dst):
        copy = pltpu.make_async_copy(src, dst, load_sem.at[len(loads)])
        copy.start()
        loads.append(copy)
        return copy

    own_cols = pl.ds(pl.multiple_of(c * half, half), half)
    other_cols = pl.ds(pl.multiple_of(other * half, half), half)
    l_routes = load(routes_h, names.at[zl])
    l_gates = load(gates_h, gates.at[zl])
    l_ctx = load(ctx_h, ctx)
    l_ow1 = load(ow_h.at[:, other_cols], ow.at[0])
    l_ow0 = load(ow_h.at[:, own_cols], ow.at[1])
    l_res = load(res_h.at[pl.ds(pl.multiple_of(zh * blk, blk), blk), own_cols], res)
    l_gain = load(gain_h, gain)
    l_gw = load(gw_h, wgu.at[:, pl.ds(0, ffn)])
    l_uw = load(uw_h, wgu.at[:, pl.ds(ffn, ffn)])
    l_dw = load(dw_h, wd)

    peer = lax.broadcasted_iota(jnp.int32, (PEERS, group), 0)
    px, py = (x + (peer >> 2)) & (NX - 1), (y + (peer & (NY - 1))) & (NY - 1)
    named = ((px * 2 + zl) * NY + py) * NHI + zh

    def slots_of(g, before):
        hit = jnp.zeros((PEERS, group), F32)
        weight = jnp.zeros((PEERS, group), F32)
        for k in range(names.shape[1]):
            same = names[g, k : k + 1, :] == named
            hit = hit + jnp.where(same, 1.0, 0.0)
            weight = weight + jnp.where(same, gates[g, k : k + 1, :], 0.0)
        earlier = (
            lax.broadcasted_iota(jnp.int32, (group, group), 0)
            < lax.broadcasted_iota(jnp.int32, (group, group), 1)
        ).astype(F32).astype(BF)
        rank = dot(hit.astype(BF), earlier) + before
        rank = jnp.where(hit > 0.0, rank, -1.0)
        slot = lax.broadcasted_iota(jnp.int32, (PEERS, SLOTS, group), 1).astype(F32)
        chosen = slot == rank[:, None, :]
        span = pl.ds(pl.multiple_of(g * group, group), group)
        pick[:, span] = jnp.where(chosen, 1.0, 0.0).reshape(ROWS, group).astype(BF)
        gated = jnp.where(chosen, jnp.broadcast_to(weight[:, None, :], chosen.shape), 0.0)
        spread[span, :] = gated.reshape(ROWS, group).T.astype(BF)
        return before + jnp.sum(hit, axis=1, keepdims=True)

    l_routes.wait()
    l_gates.wait()
    before = slots_of(zl, jnp.zeros((PEERS, 1), F32))

    l_ctx.wait()
    l_ow1.wait()
    for q, (k0, w) in enumerate(OUT):
        hp_send[:, k0 : k0 + w] = dot(ctx[...], ow[0, :, k0 : k0 + w]).astype(BF)
    l_ow0.wait()
    for q, (k0, w) in enumerate(OUT):
        total[:, k0 : k0 + w] = dot(ctx[...], ow[1, :, k0 : k0 + w])
    pl.semaphore_wait(barrier, PEERS + len(RING))
    hp_copies = []
    for q, (k0, w) in enumerate(OUT):
        cols = pl.ds(k0, w)
        hp_copies.append(send(hp_send.at[:, cols], hp_recv.at[:, cols], hp_ss.at[q], hp_rs.at[q], core))
    tables = [
        send(names.at[zl], names.at[zl], table_ss.at[0], table_rs.at[0], mate),
        send(gates.at[zl], gates.at[zl], table_ss.at[1], table_rs.at[1], mate),
    ]

    def rows_of(k):
        return pl.ds(pl.multiple_of(((zh + k + NHI) % NHI) * blk, blk), blk)

    relays, lasts = {}, {}

    def reduce_first(q):
        k0, w = OUT[q]
        cols = pl.ds(k0, w)
        way = ways[q % 2]
        hp_copies[q].wait_recv()
        total[:, cols] = total[:, cols] + hp_recv[:, cols].astype(F32)
        rs_send[0, :, cols] = total[rows_of(2), cols].astype(BF)
        relays[q] = send(rs_send.at[0, :, cols], rs_relay.at[:, cols], rs_ss.at[q, 0], relay_rs.at[q], at_z(2 * way))

    def reduce_direct(q):
        k0, w = OUT[q]
        cols = pl.ds(k0, w)
        way = ways[q % 2]
        rs_send[1, :, cols] = total[rows_of(-way), cols].astype(BF)
        lasts[q, 1] = send(
            rs_send.at[1, :, cols], rs_last.at[1, :, cols], rs_ss.at[q, 1], last_rs.at[q, 1], at_z(-2 * way)
        )

    def reduce_second(q):
        k0, w = OUT[q]
        cols = pl.ds(k0, w)
        way = ways[q % 2]
        relays[q].wait_recv()
        rs_send[2, :, cols] = (total[rows_of(way), cols] + rs_relay[:, cols].astype(F32)).astype(BF)
        lasts[q, 0] = send(
            rs_send.at[2, :, cols], rs_last.at[0, :, cols], rs_ss.at[q, 2], last_rs.at[q, 0], at_z(2 * way)
        )

    for q in range(len(OUT)):
        reduce_first(q)
    for q in range(len(OUT)):
        reduce_direct(q)

    for copy in tables:
        copy.wait_recv()
    slots_of(1 - zl, before)

    l_gain.wait()
    l_gw.wait()
    l_uw.wait()
    diagonal = lax.broadcasted_iota(jnp.int32, (128, 128), 0) == lax.broadcasted_iota(jnp.int32, (128, 128), 1)

    def fold(r, carry):
        column = jnp.sum(jnp.where(diagonal, gain[pl.ds(r, 1), :], 0.0), axis=1, keepdims=True)
        span = pl.ds(pl.multiple_of(r * 128, 128), 128)
        wgu[span, :] = (wgu[span, :].astype(F32) * column).astype(BF)
        return carry

    lax.fori_loop(0, gain.shape[0], fold, 0)
    for q in range(len(OUT)):
        reduce_second(q)

    l_res.wait()

    gathers = {}
    packs = {}

    def in_order(stages, count, steps):
        todo = []
        for q in range(count):
            lags = {1: (0, 0, 0, 1.1), 2: (0, 1.1, 1.1, 2.2), 3: (0, 1.1, 2.2, 3.3)}[steps[q]]
            todo += [(q + lag, q, n) for n, lag in enumerate(lags)]
        for _, q, n in sorted(todo, key=lambda item: (item[0], item[2])):
            stages[n](q)

    def opposite(q, d):
        return q % 2 == d

    def to_peers(src, dst, ss, rs, q, cols, sign):
        def one(i, carry):
            span = pl.ds(i * SLABS, SLABS)
            pltpu.make_async_remote_copy(
                src_ref=src.at[span, :, cols],
                dst_ref=dst.at[span, :, cols],
                send_sem=ss.at[q], recv_sem=rs.at[q],
                device_id=at_xy(i, sign), device_id_type=MESH,
            ).start()
            return carry

        for i in range(1, PEERS):
            one(i, 0)
        rest = pl.ds(SLABS, (PEERS - 1) * SLABS)
        copy = pltpu.make_async_remote_copy(
            src_ref=src.at[rest, :, cols], dst_ref=dst.at[rest, :, cols],
            send_sem=ss.at[q], recv_sem=rs.at[q],
            device_id=at_xy(1, sign), device_id_type=MESH,
        )
        sent.append(copy)
        return copy

    def spread_own(q):
        k0, w = OUT[q]
        cols = pl.ds(k0, w)
        lasts[q, 1].wait_recv()
        lasts[q, 0].wait_recv()
        summed = total[rows_of(0), cols] + rs_last[0, :, cols].astype(F32) + rs_last[1, :, cols].astype(F32)
        toks[place(0), :, cols] = (res[:, cols].astype(F32) + summed).astype(BF)
        block = toks.at[place(0), :, cols]
        if q in OUT_DIRECT:
            at = OUT_DIRECT.index(q)
            for i in reversed(range(len(RING))):
                gathers[q, i] = send(block, block, all_ss.at[at, i], all_rs.at[at, i], at_z(RING[i]))
            return
        for n in (2, 1) if OUT_STEPS[q] == 2 else (1,):
            for d, way in enumerate(ways):
                gathers[q, d, n] = send(
                    block, block, near_ss.at[q, d, n - 1], near_rs.at[q, d, n - 1], at_z(n * way)
                )

    def pass_near(q):
        if OUT_STEPS[q] != 3:
            return
        k0, w = OUT[q]
        for d, way in enumerate(ways):
            gathers[q, d, 1].wait_recv()
            block = toks.at[place(-way), :, pl.ds(k0, w)]
            gathers[q, d, 2] = send(block, block, near_ss.at[q, d, 1], near_rs.at[q, d, 1], at_z(way))

    def pass_on(q):
        if q in OUT_DIRECT:
            return
        k0, w = OUT[q]
        for d, way in enumerate(ways):
            gathers[q, d, 2].wait_recv()
            block = toks.at[place(-2 * way), :, pl.ds(k0, w)]
            for n in (2, 1) if opposite(q, d) else (1,):
                gathers[q, d, 2 + n] = send(
                    block, block, far_ss.at[q, d, n - 1], far_rs.at[q, d, n - 1], at_z(n * way)
                )

    def dispatch(q):
        k0, w = OUT[q]
        cols = pl.ds(k0, w)
        if q in OUT_DIRECT:
            for i in range(len(RING)):
                gathers[q, i].wait_recv()
        else:
            for d in range(2):
                if OUT_STEPS[q] == 2:
                    gathers[q, d, 1].wait_recv()
                for n in (3, 4) if opposite(q, d) else (3,):
                    gathers[q, d, n].wait_recv()
        picked = dot(pick[...], toks[:, :, cols].reshape(2 * group, w)).astype(BF)
        picked = picked.reshape(PEERS * SLABS, 8, w)
        rows_own[0:SLABS, :, cols] = picked[0:SLABS]
        pack[SLABS:, :, cols] = picked[SLABS:]
        packs[q] = to_peers(pack, rows_own, pack_ss, pack_rs, q, cols, 1)

    in_order((spread_own, pass_near, pass_on, dispatch), len(OUT), OUT_STEPS)

    def into(rows, q, side, first=False):
        k0, w = OUT[q]
        got = rows[:, :, k0 : k0 + w].reshape(ROWS, w)
        at = pl.multiple_of(side * half + k0, 128)
        product = dot(got, wgu[pl.ds(at, w), :])
        acc[...] = product if first else acc[...] + product
        wide = got.astype(F32)
        wide = wide * wide
        parts = [wide[:, n : n + 128] for n in range(0, w, 128)]
        if not first:
            parts.append(square[...])
        square[...] = functools.reduce(lambda a, b: a + b, parts)

    swaps = {}
    for q, (k0, w) in enumerate(OUT):
        packs[q].wait_recv()
        cols = pl.ds(k0, w)
        swaps[q] = send(rows_own.at[:, :, cols], rows_other.at[:, :, cols], swap_ss.at[q], swap_rs.at[q], core)
        into(rows_own, q, c, q == 0)
        if q:
            swaps[q - 1].wait_recv()
            into(rows_other, q - 1, other)
    swaps[len(OUT) - 1].wait_recv()
    into(rows_other, len(OUT) - 1, other)
    l_dw.wait()

    mean = jnp.sum(square[...], axis=1, keepdims=True) / (2 * half)
    inverse = lax.rsqrt(mean + 1e-06)
    gate = acc[:, 0:ffn] * inverse
    act[...] = (gate / (1.0 + jnp.exp(-gate)) * (acc[:, ffn : 2 * ffn] * inverse)).astype(BF)

    crossing, backs = {}, {}

    def out_of(q, side):
        k0, w = BACK[q]
        return dot(act[...], wd[:, pl.ds(pl.multiple_of(side * half + k0, 128), w)])

    def cross(q):
        k0, w = BACK[q]
        cols = pl.ds(k0, w)
        y_send[:, cols] = out_of(q, other).astype(BF)
        crossing[q] = send(y_send.at[:, cols], y_recv.at[:, cols], y_ss.at[q], y_rs.at[q], core)

    cross(0)
    for q, (k0, w) in enumerate(BACK):
        if q + 1 < len(BACK):
            cross(q + 1)
        cols = pl.ds(k0, w)
        own = out_of(q, c)
        crossing[q].wait_recv()
        both = (own + y_recv[:, cols].astype(F32)).astype(BF).reshape(PEERS * SLABS, 8, w)
        ret[0:SLABS, :, cols] = both[0:SLABS]
        back[SLABS:, :, cols] = both[SLABS:]
        backs[q] = to_peers(back, ret, back_ss, back_rs, q, cols, -1)

    sums = {}

    few = blk // 2
    keep = pl.ds(pl.multiple_of(c * few, few), few)
    give = pl.ds(pl.multiple_of(other * few, few), few)
    ends = {}

    def combine(q):
        k0, w = BACK[q]
        cols = pl.ds(k0, w)
        backs[q].wait_recv()
        part[:, :, cols] = dot(spread[...], ret[:, :, cols].reshape(ROWS, w)).reshape(NZ, blk, w)
        if q in BACK_DIRECT:
            at = BACK_DIRECT.index(q)
            for i in reversed(range(len(RING))):
                all_send[i, :, cols] = part[place(RING[i]), :, cols].astype(BF)
                sums[q, i] = send(
                    all_send.at[i, :, cols], all_recv.at[i, :, cols],
                    allsum_ss.at[at, i], allsum_rs.at[at, i], at_z(RING[i]),
                )
            return
        for d, way in enumerate(ways):
            for n in (2, 1) if opposite(q, d) else (1,):
                far_send[d, n - 1, :, cols] = part[place((2 + n) * way), :, cols].astype(BF)
                sums[q, d, 2 + n] = send(
                    far_send.at[d, n - 1, :, cols], far_recv.at[d, n - 1, :, cols],
                    farsum_ss.at[q, d, n - 1], farsum_rs.at[q, d, n - 1], at_z(n * way),
                )
        for d, way in enumerate(ways) if BACK_STEPS[q] == 2 else ():
            near_send[d, 0, :, cols] = part[place(way), :, cols].astype(BF)
            sums[q, d, 1] = send(
                near_send.at[d, 0, :, cols], near_recv.at[d, 0, :, cols],
                nearsum_ss.at[q, d, 0], nearsum_rs.at[q, d, 0], at_z(way),
            )

    def add_on(q):
        if q in BACK_DIRECT:
            return
        far = 1 if BACK_STEPS[q] == 3 else 2
        k0, w = BACK[q]
        cols = pl.ds(k0, w)
        for d, way in enumerate(ways):
            value = part[place(2 * way), :, cols]
            for n in (2, 1) if opposite(q, d) else (1,):
                sums[q, d, 2 + n].wait_recv()
                value = value + far_recv[d, n - 1, :, cols].astype(F32)
            near_send[d, 1, :, cols] = value.astype(BF)
            sums[q, d, 2] = send(
                near_send.at[d, 1, :, cols], near_recv.at[d, 1, :, cols],
                nearsum_ss.at[q, d, 1], nearsum_rs.at[q, d, 1], at_z(far * way),
            )

    def add_near(q):
        if BACK_STEPS[q] != 3:
            return
        k0, w = BACK[q]
        cols = pl.ds(k0, w)
        for d, way in enumerate(ways):
            sums[q, d, 2].wait_recv()
            value = part[place(way), :, cols] + near_recv[d, 1, :, cols].astype(F32)
            near_send[d, 0, :, cols] = value.astype(BF)
            sums[q, d, 1] = send(
                near_send.at[d, 0, :, cols], near_recv.at[d, 0, :, cols],
                nearsum_ss.at[q, d, 0], nearsum_rs.at[q, d, 0], at_z(way),
            )

    def finish(q):
        k0, w = BACK[q]
        cols = pl.ds(k0, w)
        value = part[place(0), :, cols]
        if q in BACK_DIRECT:
            for i in range(len(RING)):
                sums[q, i].wait_recv()
                value = value + all_recv[i, :, cols].astype(F32)
        else:
            for d in range(2):
                for n in (1, 2) if BACK_STEPS[q] == 2 else (1,):
                    sums[q, d, n].wait_recv()
                    value = value + near_recv[d, n - 1, :, cols].astype(F32)
        fin[:, cols] = (toks[place(0), :, cols].astype(F32) + value).astype(BF)
        fin_send[:, cols] = fin[give, cols]
        ends[q] = send(fin_send.at[:, cols], fin_recv.at[:, cols], fin_ss.at[q], fin_rs.at[q], core)
        out_ref[:, pl.ds(pl.multiple_of(c * half + k0, 128), w)] = fin[keep, cols]

    in_order((combine, add_on, add_near, finish), len(BACK), BACK_STEPS)

    for q, (k0, w) in enumerate(BACK):
        ends[q].wait_recv()
        out_ref[:, pl.ds(pl.multiple_of(other * half + k0, 128), w)] = fin_recv[:, k0 : k0 + w]
    for copy in sent:
        copy.wait_send()


def local(context, output_weight, residual, norm_gain, routes, gate_values, gate_weight, up_weight, down_weight):
    group, heads = context.shape
    width = residual.shape[1]
    half = width // 2
    blk = group // NHI
    ffn = gate_weight.shape[1]
    topk = routes.shape[1]
    dma = pltpu.SemaphoreType.DMA
    vm = pltpu.VMEM
    q, p = len(OUT), len(BACK)
    slabs = PEERS * SLABS
    scratch = [
        vm((group, heads), BF), vm((2, heads, half), BF), vm((blk, half), BF), vm((width // 128, 128), F32),
        vm((width, 2 * ffn), BF), vm((ffn, width), BF), dma((10,)),
        vm((group, half), BF), vm((group, half), BF), dma((q,)), dma((q,)), vm((group, half), F32),
        vm((3, blk, half), BF), vm((blk, half), BF), vm((2, blk, half), BF), dma((q, 3)), dma((q,)), dma((q, 2)),
        vm((2, topk, group), jnp.int32), vm((2, topk, group), F32), dma((2,)), dma((2,)),
        vm((ROWS, 2 * group), BF), vm((2 * group, ROWS), BF),
        vm((NZ, blk, half), BF), dma((q, 2, 2)), dma((q, 2, 2)), dma((q, 2, 2)), dma((q, 2, 2)),
        dma((max(1, len(OUT_DIRECT)), len(RING))), dma((max(1, len(OUT_DIRECT)), len(RING))),
        vm((slabs, 8, half), BF), vm((slabs, 8, half), BF), vm((slabs, 8, half), BF),
        dma((q,)), dma((q,)), dma((q,)), dma((q,)),
        vm((ROWS, 2 * ffn), F32), vm((ROWS, 128), F32), vm((ROWS, ffn), BF),
        vm((ROWS, half), BF), vm((ROWS, half), BF), dma((p,)), dma((p,)),
        vm((slabs, 8, half), BF), vm((slabs, 8, half), BF), dma((p,)), dma((p,)),
        vm((NZ, blk, half), F32),
        vm((2, 2, blk, half), BF), vm((2, 2, blk, half), BF), dma((p, 2, 2)), dma((p, 2, 2)),
        vm((2, 2, blk, half), BF), vm((2, 2, blk, half), BF), dma((p, 2, 2)), dma((p, 2, 2)),
        vm((len(RING), blk, half), BF), vm((len(RING), blk, half), BF),
        dma((max(1, len(BACK_DIRECT)), len(RING))), dma((max(1, len(BACK_DIRECT)), len(RING))),
        vm((blk, half), BF), vm((blk // 2, half), BF), vm((blk // 2, half), BF), dma((p,)), dma((p,)),
    ]
    return pl.pallas_call(
        kernel,
        out_shape=jax.ShapeDtypeStruct((blk // 2, width), BF),
        in_specs=[pl.BlockSpec(memory_space=pl.ANY)] * 9,
        out_specs=pl.BlockSpec(memory_space=pltpu.VMEM),
        scratch_shapes=scratch,
        compiler_params=pltpu.CompilerParams(
            collective_id=0, has_side_effects=True, vmem_limit_bytes=56 * 2**20
        ),
        cost_estimate=pl.CostEstimate(flops=4 * 10**9, bytes_accessed=10**7, transcendentals=0),
    )(context, output_weight, residual, norm_gain.reshape(-1, 128), routes.T, gate_values.T, gate_weight, up_weight, down_weight)


def solution(mesh):
    in_specs = (
        P("expert", "tensor"),
        P("tensor", None),
        P("expert", None),
        P(),
        P("expert", None),
        P("expert", None),
        P(None, ("expert", "tensor")),
        P(None, ("expert", "tensor")),
        P(("expert", "tensor"), None),
    )
    out_specs = P(("expert", "tensor"), None)
    return jax.shard_map(local, mesh=mesh, in_specs=in_specs, out_specs=out_specs, check_vma=False)
```

```python
import functools

import jax
import jax.numpy as jnp
from jax import lax
from jax.experimental import pallas as pl
from jax.experimental.pallas import tpu as pltpu
from jax.sharding import PartitionSpec as P

MESH = pl.DeviceIdType.MESH
NX, NY, NZ, NHI = 4, 4, 8, 4
PEERS = NX * NY
SLABS = 5
SLOTS = SLABS * 8
ROWS = PEERS * SLOTS
OUT = ((0, 128), (128, 256), (384, 256), (640, 256), (896, 128))
BACK = ((0, 128), (128, 256), (384, 256), (640, 256), (896, 128))
OUT_STEPS = (2, 2, 2, 2, 2)
BACK_STEPS = (3, 3, 3, 2, 1)
OUT_DIRECT = [q for q, n in enumerate(OUT_STEPS) if n == 1]
BACK_DIRECT = [q for q, n in enumerate(BACK_STEPS) if n == 1]
RING = (1, -1, 2, -2, 3, -3, 4)
BF, F32 = jnp.bfloat16, jnp.float32


def dot(a, b):
    return jnp.dot(a, b, preferred_element_type=F32)


def kernel(
    ctx_h, ow_h, res_h, gain_h, routes_h, gates_h, gw_h, uw_h, dw_h, out_ref,
    ctx, ow, res, gain, wgu, wd, load_sem,
    hp_send, hp_recv, hp_ss, hp_rs, total,
    rs_send, rs_relay, rs_last, rs_ss, relay_rs, last_rs,
    names, gates, table_ss, table_rs, pick, spread,
    toks, near_ss, near_rs, far_ss, far_rs, all_ss, all_rs,
    pack, rows_own, rows_other, pack_ss, pack_rs, swap_ss, swap_rs,
    acc, square, act, y_send, y_recv, y_ss, y_rs,
    back, ret, back_ss, back_rs,
    part, far_send, far_recv, farsum_ss, farsum_rs, near_send, near_recv, nearsum_ss, nearsum_rs,
    all_send, all_recv, allsum_ss, allsum_rs,
    fin, fin_send, fin_recv, fin_ss, fin_rs,
):
    e, t = lax.axis_index("expert"), lax.axis_index("tensor")
    x, zl, y = e // (2 * NY), (e // NY) % 2, e % NY
    zh, c = t // 2, t % 2
    z = zh * 2 + zl
    group = ctx.shape[0]
    half = res.shape[1]
    blk = group // NHI
    other = 1 - c
    ffn = gw_h.shape[1]
    ways = (1, -1)

    def at_z(k):
        to = (z + k + NZ) % NZ
        return {"expert": (x * 2 + to % 2) * NY + y, "tensor": (to // 2) * 2 + c}

    def at_xy(i, sign):
        px = (x + sign * (i // NY) + NX) % NX
        py = (y + sign * (i % NY) + NY) % NY
        return {"expert": (px * 2 + zl) * NY + py, "tensor": t}

    core = {"expert": e, "tensor": zh * 2 + other}
    mate = {"expert": (x * 2 + (1 - zl)) * NY + y, "tensor": t}

    def place(k):
        to = (z + k + NZ) % NZ
        return (to % 2) * NHI + to // 2

    def send(src, dst, ss, rs, to):
        copy = pltpu.make_async_remote_copy(
            src_ref=src, dst_ref=dst, send_sem=ss, recv_sem=rs, device_id=to, device_id_type=MESH
        )
        copy.start()
        sent.append(copy)
        return copy

    sent = []

    barrier = pltpu.get_barrier_semaphore()
    for to in [at_xy(i, 1) for i in range(PEERS - 1, 0, -1)] + [at_z(k) for k in reversed(RING)] + [core]:
        pl.semaphore_signal(barrier, inc=1, device_id=to, device_id_type=MESH)
    loads = []

    def load(src, dst):
        copy = pltpu.make_async_copy(src, dst, load_sem.at[len(loads)])
        copy.start()
        loads.append(copy)
        return copy

    own_cols = pl.ds(pl.multiple_of(c * half, half), half)
    other_cols = pl.ds(pl.multiple_of(other * half, half), half)
    l_routes = load(routes_h, names.at[zl])
    l_gates = load(gates_h, gates.at[zl])
    l_ctx = load(ctx_h, ctx)
    l_ow1 = load(ow_h.at[:, other_cols], ow.at[0])
    l_ow0 = load(ow_h.at[:, own_cols], ow.at[1])
    l_res = load(res_h.at[pl.ds(pl.multiple_of(zh * blk, blk), blk), own_cols], res)
    l_gain = load(gain_h, gain)
    l_gw = load(gw_h, wgu.at[:, pl.ds(0, ffn)])
    l_uw = load(uw_h, wgu.at[:, pl.ds(ffn, ffn)])
    l_dw = load(dw_h, wd)

    peer = lax.broadcasted_iota(jnp.int32, (PEERS, group), 0)
    px, py = (x + (peer >> 2)) & (NX - 1), (y + (peer & (NY - 1))) & (NY - 1)
    named = ((px * 2 + zl) * NY + py) * NHI + zh

    def slots_of(g, before):
        hit = jnp.zeros((PEERS, group), F32)
        weight = jnp.zeros((PEERS, group), F32)
        for k in range(names.shape[1]):
            same = names[g, k : k + 1, :] == named
            hit = hit + jnp.where(same, 1.0, 0.0)
            weight = weight + jnp.where(same, gates[g, k : k + 1, :], 0.0)
        earlier = (
            lax.broadcasted_iota(jnp.int32, (group, group), 0)
            < lax.broadcasted_iota(jnp.int32, (group, group), 1)
        ).astype(F32).astype(BF)
        rank = dot(hit.astype(BF), earlier) + before
        rank = jnp.where(hit > 0.0, rank, -1.0)
        slot = lax.broadcasted_iota(jnp.int32, (PEERS, SLOTS, group), 1).astype(F32)
        chosen = slot == rank[:, None, :]
        span = pl.ds(pl.multiple_of(g * group, group), group)
        pick[:, span] = jnp.where(chosen, 1.0, 0.0).reshape(ROWS, group).astype(BF)
        gated = jnp.where(chosen, jnp.broadcast_to(weight[:, None, :], chosen.shape), 0.0)
        spread[span, :] = gated.reshape(ROWS, group).T.astype(BF)
        return before + jnp.sum(hit, axis=1, keepdims=True)

    l_routes.wait()
    l_gates.wait()
    before = slots_of(zl, jnp.zeros((PEERS, 1), F32))

    l_ctx.wait()
    l_ow1.wait()
    for q, (k0, w) in enumerate(OUT):
        hp_send[:, k0 : k0 + w] = dot(ctx[...], ow[0, :, k0 : k0 + w]).astype(BF)
    l_ow0.wait()
    for q, (k0, w) in enumerate(OUT):
        total[:, k0 : k0 + w] = dot(ctx[...], ow[1, :, k0 : k0 + w])
    pl.semaphore_wait(barrier, PEERS + len(RING))
    hp_copies = []
    for q, (k0, w) in enumerate(OUT):
        cols = pl.ds(k0, w)
        hp_copies.append(send(hp_send.at[:, cols], hp_recv.at[:, cols], hp_ss.at[q], hp_rs.at[q], core))
    tables = [
        send(names.at[zl], names.at[zl], table_ss.at[0], table_rs.at[0], mate),
        send(gates.at[zl], gates.at[zl], table_ss.at[1], table_rs.at[1], mate),
    ]

    def rows_of(k):
        return pl.ds(pl.multiple_of(((zh + k + NHI) % NHI) * blk, blk), blk)

    relays, lasts = {}, {}

    def reduce_first(q):
        k0, w = OUT[q]
        cols = pl.ds(k0, w)
        way = ways[q % 2]
        hp_copies[q].wait_recv()
        total[:, cols] = total[:, cols] + hp_recv[:, cols].astype(F32)
        rs_send[0, :, cols] = total[rows_of(2), cols].astype(BF)
        relays[q] = send(rs_send.at[0, :, cols], rs_relay.at[:, cols], rs_ss.at[q, 0], relay_rs.at[q], at_z(2 * way))

    def reduce_direct(q):
        k0, w = OUT[q]
        cols = pl.ds(k0, w)
        way = ways[q % 2]
        rs_send[1, :, cols] = total[rows_of(-way), cols].astype(BF)
        lasts[q, 1] = send(
            rs_send.at[1, :, cols], rs_last.at[1, :, cols], rs_ss.at[q, 1], last_rs.at[q, 1], at_z(-2 * way)
        )

    def reduce_second(q):
        k0, w = OUT[q]
        cols = pl.ds(k0, w)
        way = ways[q % 2]
        relays[q].wait_recv()
        rs_send[2, :, cols] = (total[rows_of(way), cols] + rs_relay[:, cols].astype(F32)).astype(BF)
        lasts[q, 0] = send(
            rs_send.at[2, :, cols], rs_last.at[0, :, cols], rs_ss.at[q, 2], last_rs.at[q, 0], at_z(2 * way)
        )

    for q in range(len(OUT)):
        reduce_first(q)
    for q in range(len(OUT)):
        reduce_direct(q)

    for copy in tables:
        copy.wait_recv()
    slots_of(1 - zl, before)

    l_gain.wait()
    l_gw.wait()
    l_uw.wait()
    diagonal = lax.broadcasted_iota(jnp.int32, (128, 128), 0) == lax.broadcasted_iota(jnp.int32, (128, 128), 1)

    def fold(r, carry):
        column = jnp.sum(jnp.where(diagonal, gain[pl.ds(r, 1), :], 0.0), axis=1, keepdims=True)
        span = pl.ds(pl.multiple_of(r * 128, 128), 128)
        wgu[span, :] = (wgu[span, :].astype(F32) * column).astype(BF)
        return carry

    lax.fori_loop(0, gain.shape[0], fold, 0)
    for q in range(len(OUT)):
        reduce_second(q)

    l_res.wait()

    gathers = {}
    packs = {}

    def in_order(stages, count, steps, lag):
        todo = []
        for q in range(count):
            lags = {1: (0, 0, 0, 2 * lag), 2: (0, lag, lag, 2 * lag), 3: (0, lag, 2 * lag, 9)}[steps[q]]
            todo += [(q + lag, q, n) for n, lag in enumerate(lags)]
        for _, q, n in sorted(todo, key=lambda item: (item[0], item[2])):
            stages[n](q)

    def opposite(q, d):
        return q % 2 == d

    def to_peers(src, dst, ss, rs, q, cols, sign):
        def one(i, carry):
            span = pl.ds(i * SLABS, SLABS)
            pltpu.make_async_remote_copy(
                src_ref=src.at[span, :, cols],
                dst_ref=dst.at[span, :, cols],
                send_sem=ss.at[q], recv_sem=rs.at[q],
                device_id=at_xy(i, sign), device_id_type=MESH,
            ).start()
            return carry

        for i in range(1, PEERS):
            one(i, 0)
        rest = pl.ds(SLABS, (PEERS - 1) * SLABS)
        copy = pltpu.make_async_remote_copy(
            src_ref=src.at[rest, :, cols], dst_ref=dst.at[rest, :, cols],
            send_sem=ss.at[q], recv_sem=rs.at[q],
            device_id=at_xy(1, sign), device_id_type=MESH,
        )
        sent.append(copy)
        return copy

    def spread_own(q):
        k0, w = OUT[q]
        cols = pl.ds(k0, w)
        lasts[q, 1].wait_recv()
        lasts[q, 0].wait_recv()
        summed = total[rows_of(0), cols] + rs_last[0, :, cols].astype(F32) + rs_last[1, :, cols].astype(F32)
        toks[place(0), :, cols] = (res[:, cols].astype(F32) + summed).astype(BF)
        block = toks.at[place(0), :, cols]
        if q in OUT_DIRECT:
            at = OUT_DIRECT.index(q)
            for i in reversed(range(len(RING))):
                gathers[q, i] = send(block, block, all_ss.at[at, i], all_rs.at[at, i], at_z(RING[i]))
            return
        for n in (2, 1) if OUT_STEPS[q] == 2 else (1,):
            for d, way in enumerate(ways):
                gathers[q, d, n] = send(
                    block, block, near_ss.at[q, d, n - 1], near_rs.at[q, d, n - 1], at_z(n * way)
                )

    def pass_near(q):
        if OUT_STEPS[q] != 3:
            return
        k0, w = OUT[q]
        for d, way in enumerate(ways):
            gathers[q, d, 1].wait_recv()
            block = toks.at[place(-way), :, pl.ds(k0, w)]
            gathers[q, d, 2] = send(block, block, near_ss.at[q, d, 1], near_rs.at[q, d, 1], at_z(way))

    def pass_on(q):
        if q in OUT_DIRECT:
            return
        k0, w = OUT[q]
        for d, way in enumerate(ways):
            gathers[q, d, 2].wait_recv()
            block = toks.at[place(-2 * way), :, pl.ds(k0, w)]
            for n in (2, 1) if opposite(q, d) else (1,):
                gathers[q, d, 2 + n] = send(
                    block, block, far_ss.at[q, d, n - 1], far_rs.at[q, d, n - 1], at_z(n * way)
                )

    def dispatch(q):
        k0, w = OUT[q]
        cols = pl.ds(k0, w)
        if q in OUT_DIRECT:
            for i in range(len(RING)):
                gathers[q, i].wait_recv()
        else:
            for d in range(2):
                if OUT_STEPS[q] == 2:
                    gathers[q, d, 1].wait_recv()
                for n in (3, 4) if opposite(q, d) else (3,):
                    gathers[q, d, n].wait_recv()
        picked = dot(pick[...], toks[:, :, cols].reshape(2 * group, w)).astype(BF)
        picked = picked.reshape(PEERS * SLABS, 8, w)
        rows_own[0:SLABS, :, cols] = picked[0:SLABS]
        pack[SLABS:, :, cols] = picked[SLABS:]
        packs[q] = to_peers(pack, rows_own, pack_ss, pack_rs, q, cols, 1)

    in_order((spread_own, pass_near, pass_on, dispatch), len(OUT), OUT_STEPS, 1.1)

    def into(rows, q, side, first=False):
        k0, w = OUT[q]
        got = rows[:, :, k0 : k0 + w].reshape(ROWS, w)
        at = pl.multiple_of(side * half + k0, 128)
        product = dot(got, wgu[pl.ds(at, w), :])
        acc[...] = product if first else acc[...] + product
        wide = got.astype(F32)
        wide = wide * wide
        parts = [wide[:, n : n + 128] for n in range(0, w, 128)]
        if not first:
            parts.append(square[...])
        square[...] = functools.reduce(lambda a, b: a + b, parts)

    swaps = {}
    for q, (k0, w) in enumerate(OUT):
        packs[q].wait_recv()
        cols = pl.ds(k0, w)
        swaps[q] = send(rows_own.at[:, :, cols], rows_other.at[:, :, cols], swap_ss.at[q], swap_rs.at[q], core)
        into(rows_own, q, c, q == 0)
        if q:
            swaps[q - 1].wait_recv()
            into(rows_other, q - 1, other)
    swaps[len(OUT) - 1].wait_recv()
    into(rows_other, len(OUT) - 1, other)
    l_dw.wait()

    mean = jnp.sum(square[...], axis=1, keepdims=True) / (2 * half)
    inverse = lax.rsqrt(mean + 1e-06)
    gate = acc[:, 0:ffn] * inverse
    act[...] = (gate / (1.0 + jnp.exp(-gate)) * (acc[:, ffn : 2 * ffn] * inverse)).astype(BF)

    crossing, backs = {}, {}

    def out_of(q, side):
        k0, w = BACK[q]
        return dot(act[...], wd[:, pl.ds(pl.multiple_of(side * half + k0, 128), w)])

    def cross(q):
        k0, w = BACK[q]
        cols = pl.ds(k0, w)
        y_send[:, cols] = out_of(q, other).astype(BF)
        crossing[q] = send(y_send.at[:, cols], y_recv.at[:, cols], y_ss.at[q], y_rs.at[q], core)

    cross(0)
    for q, (k0, w) in enumerate(BACK):
        if q + 1 < len(BACK):
            cross(q + 1)
        cols = pl.ds(k0, w)
        own = out_of(q, c)
        crossing[q].wait_recv()
        both = (own + y_recv[:, cols].astype(F32)).astype(BF).reshape(PEERS * SLABS, 8, w)
        ret[0:SLABS, :, cols] = both[0:SLABS]
        back[SLABS:, :, cols] = both[SLABS:]
        backs[q] = to_peers(back, ret, back_ss, back_rs, q, cols, -1)

    sums = {}

    few = blk // 2
    keep = pl.ds(pl.multiple_of(c * few, few), few)
    give = pl.ds(pl.multiple_of(other * few, few), few)
    ends = {}

    def combine(q):
        k0, w = BACK[q]
        cols = pl.ds(k0, w)
        backs[q].wait_recv()
        part[:, :, cols] = dot(spread[...], ret[:, :, cols].reshape(ROWS, w)).reshape(NZ, blk, w)
        if q in BACK_DIRECT:
            at = BACK_DIRECT.index(q)
            for i in reversed(range(len(RING))):
                all_send[i, :, cols] = part[place(RING[i]), :, cols].astype(BF)
                sums[q, i] = send(
                    all_send.at[i, :, cols], all_recv.at[i, :, cols],
                    allsum_ss.at[at, i], allsum_rs.at[at, i], at_z(RING[i]),
                )
            return
        for d, way in enumerate(ways):
            for n in (2, 1) if opposite(q, d) else (1,):
                far_send[d, n - 1, :, cols] = part[place((2 + n) * way), :, cols].astype(BF)
                sums[q, d, 2 + n] = send(
                    far_send.at[d, n - 1, :, cols], far_recv.at[d, n - 1, :, cols],
                    farsum_ss.at[q, d, n - 1], farsum_rs.at[q, d, n - 1], at_z(n * way),
                )
        for d, way in enumerate(ways) if BACK_STEPS[q] == 2 else ():
            near_send[d, 0, :, cols] = part[place(way), :, cols].astype(BF)
            sums[q, d, 1] = send(
                near_send.at[d, 0, :, cols], near_recv.at[d, 0, :, cols],
                nearsum_ss.at[q, d, 0], nearsum_rs.at[q, d, 0], at_z(way),
            )

    def add_on(q):
        if q in BACK_DIRECT:
            return
        far = 1 if BACK_STEPS[q] == 3 else 2
        k0, w = BACK[q]
        cols = pl.ds(k0, w)
        for d, way in enumerate(ways):
            value = part[place(2 * way), :, cols]
            for n in (2, 1) if opposite(q, d) else (1,):
                sums[q, d, 2 + n].wait_recv()
                value = value + far_recv[d, n - 1, :, cols].astype(F32)
            near_send[d, 1, :, cols] = value.astype(BF)
            sums[q, d, 2] = send(
                near_send.at[d, 1, :, cols], near_recv.at[d, 1, :, cols],
                nearsum_ss.at[q, d, 1], nearsum_rs.at[q, d, 1], at_z(far * way),
            )

    def add_near(q):
        if BACK_STEPS[q] != 3:
            return
        k0, w = BACK[q]
        cols = pl.ds(k0, w)
        for d, way in enumerate(ways):
            sums[q, d, 2].wait_recv()
            value = part[place(way), :, cols] + near_recv[d, 1, :, cols].astype(F32)
            near_send[d, 0, :, cols] = value.astype(BF)
            sums[q, d, 1] = send(
                near_send.at[d, 0, :, cols], near_recv.at[d, 0, :, cols],
                nearsum_ss.at[q, d, 0], nearsum_rs.at[q, d, 0], at_z(way),
            )

    def finish(q):
        k0, w = BACK[q]
        cols = pl.ds(k0, w)
        value = part[place(0), :, cols]
        if q in BACK_DIRECT:
            for i in range(len(RING)):
                sums[q, i].wait_recv()
                value = value + all_recv[i, :, cols].astype(F32)
        else:
            for d in range(2):
                for n in (1, 2) if BACK_STEPS[q] == 2 else (1,):
                    sums[q, d, n].wait_recv()
                    value = value + near_recv[d, n - 1, :, cols].astype(F32)
        fin[:, cols] = (toks[place(0), :, cols].astype(F32) + value).astype(BF)
        fin_send[:, cols] = fin[give, cols]
        ends[q] = send(fin_send.at[:, cols], fin_recv.at[:, cols], fin_ss.at[q], fin_rs.at[q], core)
        out_ref[:, pl.ds(pl.multiple_of(c * half + k0, 128), w)] = fin[keep, cols]

    in_order((combine, add_on, add_near, finish), len(BACK), BACK_STEPS, 1.1)

    for q, (k0, w) in enumerate(BACK):
        ends[q].wait_recv()
        out_ref[:, pl.ds(pl.multiple_of(other * half + k0, 128), w)] = fin_recv[:, k0 : k0 + w]
    for copy in sent:
        copy.wait_send()


def local(context, output_weight, residual, norm_gain, routes, gate_values, gate_weight, up_weight, down_weight):
    group, heads = context.shape
    width = residual.shape[1]
    half = width // 2
    blk = group // NHI
    ffn = gate_weight.shape[1]
    topk = routes.shape[1]
    dma = pltpu.SemaphoreType.DMA
    vm = pltpu.VMEM
    q, p = len(OUT), len(BACK)
    slabs = PEERS * SLABS
    scratch = [
        vm((group, heads), BF), vm((2, heads, half), BF), vm((blk, half), BF), vm((width // 128, 128), F32),
        vm((width, 2 * ffn), BF), vm((ffn, width), BF), dma((10,)),
        vm((group, half), BF), vm((group, half), BF), dma((q,)), dma((q,)), vm((group, half), F32),
        vm((3, blk, half), BF), vm((blk, half), BF), vm((2, blk, half), BF), dma((q, 3)), dma((q,)), dma((q, 2)),
        vm((2, topk, group), jnp.int32), vm((2, topk, group), F32), dma((2,)), dma((2,)),
        vm((ROWS, 2 * group), BF), vm((2 * group, ROWS), BF),
        vm((NZ, blk, half), BF), dma((q, 2, 2)), dma((q, 2, 2)), dma((q, 2, 2)), dma((q, 2, 2)),
        dma((max(1, len(OUT_DIRECT)), len(RING))), dma((max(1, len(OUT_DIRECT)), len(RING))),
        vm((slabs, 8, half), BF), vm((slabs, 8, half), BF), vm((slabs, 8, half), BF),
        dma((q,)), dma((q,)), dma((q,)), dma((q,)),
        vm((ROWS, 2 * ffn), F32), vm((ROWS, 128), F32), vm((ROWS, ffn), BF),
        vm((ROWS, half), BF), vm((ROWS, half), BF), dma((p,)), dma((p,)),
        vm((slabs, 8, half), BF), vm((slabs, 8, half), BF), dma((p,)), dma((p,)),
        vm((NZ, blk, half), F32),
        vm((2, 2, blk, half), BF), vm((2, 2, blk, half), BF), dma((p, 2, 2)), dma((p, 2, 2)),
        vm((2, 2, blk, half), BF), vm((2, 2, blk, half), BF), dma((p, 2, 2)), dma((p, 2, 2)),
        vm((len(RING), blk, half), BF), vm((len(RING), blk, half), BF),
        dma((max(1, len(BACK_DIRECT)), len(RING))), dma((max(1, len(BACK_DIRECT)), len(RING))),
        vm((blk, half), BF), vm((blk // 2, half), BF), vm((blk // 2, half), BF), dma((p,)), dma((p,)),
    ]
    return pl.pallas_call(
        kernel,
        out_shape=jax.ShapeDtypeStruct((blk // 2, width), BF),
        in_specs=[pl.BlockSpec(memory_space=pl.ANY)] * 9,
        out_specs=pl.BlockSpec(memory_space=pltpu.VMEM),
        scratch_shapes=scratch,
        compiler_params=pltpu.CompilerParams(
            collective_id=0, has_side_effects=True, vmem_limit_bytes=56 * 2**20
        ),
        cost_estimate=pl.CostEstimate(flops=4 * 10**9, bytes_accessed=10**7, transcendentals=0),
    )(context, output_weight, residual, norm_gain.reshape(-1, 128), routes.T, gate_values.T, gate_weight, up_weight, down_weight)


def solution(mesh):
    in_specs = (
        P("expert", "tensor"),
        P("tensor", None),
        P("expert", None),
        P(),
        P("expert", None),
        P("expert", None),
        P(None, ("expert", "tensor")),
        P(None, ("expert", "tensor")),
        P(("expert", "tensor"), None),
    )
    out_specs = P(("expert", "tensor"), None)
    return jax.shard_map(local, mesh=mesh, in_specs=in_specs, out_specs=out_specs, check_vma=False)
```
